32 devices in a mesh: parts: 1, var: 8 (over z, core), patch: 4 (over y, x).
Axes of the slice: x: 2, y: 2, z: 4, core: 2. Of those that a mesh axis runs over, the one named last changes fastest.
Arguments:
- tokens: bfloat16 [256, 24, 768], P('patch', ('parts', 'var')), may hold values from -6 to 6
- patch_mask: int32 [256, 24], P('patch', ('parts', 'var')), may hold values 0 or 1
- group_ids: int32 [24], P('parts'), may hold values from 0 to 7, never falling along the last dimension, each value on 1 to 6 neighbouring positions
- time_gain: float32 [768], replicated, may hold values from 0.1 to 1.9
- time_qkv: bfloat16 [768, 3, 768], P(None, None, 'patch'), may hold values from -0.21875 to 0.21875
- time_out: bfloat16 [768, 768], P('patch'), may hold values from -0.21875 to 0.21875
- space_gain: float32 [768], replicated, may hold values from 0.1 to 1.9
- space_qkv: bfloat16 [768, 3, 768], P(None, None, 'patch'), may hold values from -0.21875 to 0.21875
- space_out: bfloat16 [768, 768], P('patch'), may hold values from -0.21875 to 0.21875
Outputs:
- panel_out: bfloat16 [256, 24, 768], P('patch', ('parts', 'var'))
The draws below stay inside these ranges and needn't reach their ends.
Inputs may be any that keep to these rules, and one draw needn't show every extreme that they name: group_ids never falls along the variates; each group is a run of 1 to 6 consecutive variates.
All inputs are finite; a program needn't handle non-finite values. No bound on the sum of `patch_mask` on one device may be relied on, other than what follows from the above.
Results may differ from the reference program's by a relative error of at most 0.017.
Values may be sent and summed in bfloat16 or wider, within the bound.
No kernel may reach another device: no remote copies, remote signals or barrier semaphores. Data moves between devices by JAX's collectives and lax.ppermute only.
A program may use at most 64 MiB of HBM per device.

```python
import math
import jax
import jax.numpy as jnp
import numpy as np
from jax import lax

D = 768
HEADS = 12
HD = 64
VAR_DEV = 3
V = 24
P_SIZE = 256
GMAX = 6
GROUPS = 8
N_PATCH = 4


def plant(result, key, low, top_value):
    extent = result.shape
    place = [jax.random.randint(jax.random.fold_in(key, axis), (), 0, extent[axis]) for axis in range(len(extent))]
    result = result.at[tuple(place)].set(low)
    longest = extent.index(max(extent))
    place[longest] = (place[longest] + 1) % extent[longest]
    return result.at[tuple(place)].set(top_value)


def block_levels(key, shape, cuts, least, largest):
    factor_of = 1.0
    for dim, blocks in cuts:
        draws = jax.random.uniform(jax.random.fold_in(jax.random.fold_in(key, 6), dim), (blocks,), jnp.float32, least / len(cuts), largest / len(cuts))
        factor_of = factor_of * jnp.repeat(jnp.exp(draws), shape[dim] // blocks).reshape((-1,) + (1,) * (len(shape) - 1 - dim))
    return factor_of


def split_up(number_of, total, limit, skew):
    weights = [(1 << 20) // math.isqrt(grade ** skew) + 1 for grade in range(2, number_of + 1)]
    surplus, holding = total - limit - (number_of - 1), [1] * (number_of - 1)
    while surplus > 0:
        movable = [i for i in range(number_of - 1) if holding[i] < limit]
        mass, remaining = sum([weights[i] for i in movable]), surplus
        for i in movable:
            more = min(limit - holding[i], max(1, remaining * weights[i] // mass), surplus)
            holding[i] = holding[i] + more
            surplus = surplus - more
    return np.array([limit] + holding)


def uneven(own_key, count, total, limit, skew):
    if count == 2:
        one = jax.random.randint(own_key, (), max(1, total - limit), min(limit, total - 1) + 1)
        return jnp.stack([one, total - one])
    lengths = jnp.asarray(split_up(count, total, limit, skew), jnp.int32)
    twos = (count - 1) // 2
    source_of, receiver = lengths[1:1 + 2 * twos:2], lengths[2:2 + 2 * twos:2]
    slack = jnp.minimum(source_of - 1, limit - receiver)
    shifted = jax.random.randint(jax.random.fold_in(own_key, 1), (twos,), 0, 1 << 20) % (slack + 1)
    lengths = lengths.at[1:1 + 2 * twos:2].set(source_of - shifted).at[2:2 + 2 * twos:2].set(receiver + shifted)
    return lengths[jax.random.permutation(jax.random.fold_in(own_key, 2), count)]


def normal_values(key, extent, deviation, limit, cuts=(), kind=jnp.bfloat16):
    level = block_levels(key, extent, cuts, -0.22, 0.18) if cuts else 1.0
    array = jax.random.normal(key, extent, jnp.float32) * deviation * level
    return jnp.minimum(jnp.maximum(array, -limit), limit).astype(kind)


def setup_inputs(seed: int = 0, part: int = 0) -> dict:
    keys = jax.random.split(jax.random.key(seed), 10)
    part_keys = jax.random.split(jax.random.fold_in(keys[9], part), 10)
    tokens = normal_values(part_keys[0], (P_SIZE, V, D), 1.0, 6.0, ((0, 4), (1, 8)))
    patch_mask = plant((jax.random.randint(part_keys[1], (P_SIZE, V), 0, 4) < 3).astype(jnp.int32), jax.random.fold_in(part_keys[1], 1), 0, 1)
    group_ids = jnp.searchsorted(jnp.cumsum(uneven(part_keys[2], GROUPS, V, GMAX, 2)), jnp.arange(V), side="right").astype(jnp.int32)
    time_gain = jnp.clip(1.0 + 0.18 * jax.random.normal(keys[3], (D,), jnp.float32), 0.1, 1.9)
    time_qkv = normal_values(keys[4], (D, 3, D), D ** -0.5, 0.21875, ((2, 4),))
    time_out = normal_values(keys[5], (D, D), D ** -0.5, 0.21875, ((0, 4),))
    space_gain = jnp.clip(1.0 + 0.18 * jax.random.normal(keys[6], (D,), jnp.float32), 0.1, 1.9)
    space_qkv = normal_values(keys[7], (D, 3, D), D ** -0.5, 0.21875, ((2, 4),))
    space_out = normal_values(keys[8], (D, D), D ** -0.5, 0.21875, ((0, 4),))
    return {"tokens": tokens, "patch_mask": patch_mask, "group_ids": group_ids, "time_gain": time_gain, "time_qkv": time_qkv, "time_out": time_out, "space_gain": space_gain, "space_qkv": space_qkv, "space_out": space_out}


epsilon = 1e-06

def norm_rows(block_rows, gain):
    floats = block_rows.astype(jnp.float32)
    scaled = floats * lax.rsqrt(lax.optimization_barrier(jnp.mean(floats * floats, axis=-1, keepdims=True)) + epsilon)
    return (scaled * gain.astype(jnp.float32)).astype(jnp.bfloat16)

def project(normed, weight):
    return jnp.einsum('pvd,dtk->pvtk', normed.astype(jnp.float32), weight.astype(jnp.float32)).astype(jnp.bfloat16)

def soft_weights(scores, allowed):
    masked = jnp.where(allowed, scores, -jnp.inf)
    highest = lax.optimization_barrier(jnp.max(masked, axis=-1, keepdims=True))
    raised = jnp.exp(masked - highest)
    return (raised / lax.optimization_barrier(jnp.sum(raised, axis=-1, keepdims=True))).astype(jnp.bfloat16)

def head_sum(attended, weight):
    group_width = D // N_PATCH
    lead_shape = attended.shape[:-1]
    flat = attended.reshape(-1, D)
    summed = jnp.zeros((flat.shape[0], D), jnp.float32)
    for group in range(N_PATCH):
        part = jnp.dot(flat[:, group * group_width:(group + 1) * group_width], weight[group * group_width:(group + 1) * group_width], preferred_element_type=jnp.float32)
        part = lax.optimization_barrier(part.astype(jnp.bfloat16))
        summed = summed + part.astype(jnp.float32)
    return summed.reshape(lead_shape + (D,))

def time_block(block_rows, block_mask, gain, weight, out_weight):
    patch_count, var_count = (block_rows.shape[0], block_rows.shape[1])
    projected = project(norm_rows(block_rows, gain), weight)
    queries = projected[:, :, 0].reshape(patch_count, var_count, HEADS, HD).astype(jnp.float32)
    key_rows = projected[:, :, 1].reshape(patch_count, var_count, HEADS, HD).astype(jnp.float32)
    value_rows = projected[:, :, 2].reshape(patch_count, var_count, HEADS, HD).astype(jnp.float32)
    scores = jnp.einsum('qvhe,kvhe->vhqk', queries, key_rows) * HD ** (-0.5)
    query_pos = jnp.arange(patch_count)[:, None]
    key_pos = jnp.arange(patch_count)[None, :]
    observed = (block_mask.T > 0)[:, None, None, :]
    allowed = (key_pos <= query_pos)[None, None] & (observed | (key_pos == query_pos)[None, None])
    weights = soft_weights(scores, allowed)
    attended = jnp.einsum('vhqk,kvhe->qvhe', weights.astype(jnp.float32), value_rows).astype(jnp.bfloat16)
    attended = attended.reshape(patch_count, var_count, D)
    mixed = head_sum(attended, out_weight)
    return (block_rows.astype(jnp.float32) + mixed).astype(jnp.bfloat16)

def space_block(block_rows, group_ids, gain, weight, out_weight):
    patch_count, var_count = (block_rows.shape[0], block_rows.shape[1])
    projected = project(norm_rows(block_rows, gain), weight)
    queries = projected[:, :, 0].reshape(patch_count, var_count, HEADS, HD).astype(jnp.float32)
    key_rows = projected[:, :, 1].reshape(patch_count, var_count, HEADS, HD).astype(jnp.float32)
    value_rows = projected[:, :, 2].reshape(patch_count, var_count, HEADS, HD).astype(jnp.float32)
    scores = jnp.einsum('pqhe,pkhe->phqk', queries, key_rows) * HD ** (-0.5)
    allowed = (group_ids[:, None] == group_ids[None, :])[None, None]
    weights = soft_weights(scores, allowed)
    attended = jnp.einsum('phqk,pkhe->pqhe', weights.astype(jnp.float32), value_rows).astype(jnp.bfloat16)
    attended = attended.reshape(patch_count, var_count, D)
    mixed = head_sum(attended, out_weight)
    return (block_rows.astype(jnp.float32) + mixed).astype(jnp.bfloat16)

def reference(tokens, patch_mask, group_ids, time_gain, time_qkv, time_out, space_gain, space_qkv, space_out):
    block_count = V // VAR_DEV

    def time_step(block):
        start = (block * VAR_DEV).astype(jnp.int32)
        rows_in = lax.dynamic_slice_in_dim(tokens, start, VAR_DEV, 1)
        mask_in = lax.dynamic_slice_in_dim(patch_mask, start, VAR_DEV, 1)
        return time_block(rows_in, mask_in, time_gain, time_qkv, time_out)
    middle = lax.map(time_step, jnp.arange(block_count, dtype=jnp.int32))
    middle = jnp.transpose(middle, (1, 0, 2, 3)).reshape(P_SIZE, V, D)
    patch_blocks = P_SIZE // N_PATCH

    def space_step(block):
        start = (block * N_PATCH).astype(jnp.int32)
        rows_in = lax.dynamic_slice_in_dim(middle, start, N_PATCH, 0)
        return space_block(rows_in, group_ids, space_gain, space_qkv, space_out)
    final = lax.map(space_step, jnp.arange(patch_blocks, dtype=jnp.int32))
    return final.reshape(P_SIZE, V, D)
```

```python
import functools

import jax
import jax.numpy as jnp
from jax import lax
from jax.experimental import pallas as pl
from jax.experimental.pallas import tpu as pltpu
from jax.sharding import PartitionSpec as P

HD = 64
epsilon = 1e-06
NT = (((1,), (1,)), ((), ()))
VM = pl.BlockSpec(memory_space=pltpu.VMEM)
SM = pl.BlockSpec(memory_space=pltpu.SMEM)


def params():
    return pltpu.CompilerParams(vmem_limit_bytes=28 * 1024 * 1024)


def cost(flops, size):
    return pl.CostEstimate(flops=flops, bytes_accessed=size, transcendentals=0)


def normed(floats, gain):
    mean = jnp.mean(floats * floats, axis=-1, keepdims=True)
    return (floats * lax.rsqrt(mean + epsilon) * gain).astype(jnp.bfloat16)


def dot_nt(a, b):
    return lax.dot_general(a, b, NT, preferred_element_type=jnp.float32)


def time_kernel(base_ref, t0, t1, t2, t3, mask_ref, gain_ref, w_ref, o0, o1, o2, o3):
    tokens, outs = (t0, t1, t2, t3), (o0, o1, o2, o3)
    var_count, rows, depth = t0.shape
    width = w_ref.shape[0] // 3
    total = rows * len(tokens)
    row = lax.broadcasted_iota(jnp.int32, (total, total), 0)
    col = lax.broadcasted_iota(jnp.int32, (total, total), 1)

    def positions(index):
        where = index + base_ref[0]
        for block in range(1, len(tokens)):
            shift = base_ref[block] - block * rows
            where = jnp.where(index >= block * rows, index + shift, where)
        return where

    query_pos, key_pos = positions(row), positions(col)
    causal, same = key_pos <= query_pos, key_pos == query_pos
    head_of = lax.broadcasted_iota(jnp.int32, (1, width), 1) // HD
    gain = gain_ref[...]
    weight = w_ref[...]
    for v in range(var_count):
        raw = jnp.concatenate([t[v] for t in tokens], axis=0).astype(jnp.float32)
        x = normed(raw, gain)
        projected = dot_nt(x, weight)
        queries = (projected[:, :width].astype(jnp.bfloat16)).astype(jnp.float32) * HD ** (-0.5)
        queries = queries.astype(jnp.bfloat16)
        keys = projected[:, width : 2 * width].astype(jnp.bfloat16)
        values = projected[:, 2 * width :].astype(jnp.bfloat16)
        observed = mask_ref[v : v + 1, :] > 0
        bias = jnp.where(causal & (observed | same), 0.0, -jnp.inf)
        attended = jnp.zeros((total, width), jnp.float32)
        for head in range(width // HD):
            mine = head_of == head
            scores = dot_nt(jnp.where(mine, queries, 0), keys) + bias
            raised = jnp.exp(scores - jnp.max(scores, axis=-1, keepdims=True))
            share = 1.0 / jnp.sum(raised, axis=-1, keepdims=True)
            weights = (raised * share).astype(jnp.bfloat16)
            mixed = jnp.dot(weights, values, preferred_element_type=jnp.float32)
            attended = jnp.where(mine, mixed, attended)
        attended = attended.astype(jnp.bfloat16)
        for block, out in enumerate(outs):
            out[v] = attended[block * rows : (block + 1) * rows]


def mid_kernel(
    place_ref, a0, a1, a2, a3, w0, w1, w2, wa, wb, tok_ref, gain_ref, mid_ref, x_ref, f1_ref, f2_ref, last
):
    half = wa.shape[0]
    core = place_ref[0]
    last[pl.ds(pl.multiple_of(core * half, 32), half), :] = wa[...]
    last[pl.ds(pl.multiple_of((1 - core) * half, 32), half), :] = wb[...]
    var_count, rows, depth = tok_ref.shape
    gain = gain_ref[...]
    for v in range(var_count):
        summed = jnp.dot(a0[v], w0[...], preferred_element_type=jnp.float32)
        for a, w in ((a1, w1), (a2, w2), (a3, last)):
            summed = summed + jnp.dot(a[v], w[...], preferred_element_type=jnp.float32)
        mid = (tok_ref[v].astype(jnp.float32) + summed).astype(jnp.bfloat16)
        mid_ref[v] = mid
        x_ref[v] = normed(mid.astype(jnp.float32), gain)
    far = f1_ref.shape[0]
    f1_ref[...] = x_ref[pl.ds(place_ref[1], far)]
    f2_ref[...] = x_ref[pl.ds(place_ref[2], far)]


def space_kernel(
    place_ref, ids_ref,
    x0, xs, xo, f1, f2, mid_ref,
    w0, w1, w2, wa, wb, u0, u1, u2, ua, ub,
    out_ref,
    far, wall, uall, qbuf, kbuf, vbuf, prob, att,
):
    var_count, rows, depth = x0.shape
    far_count = f1.shape[0]
    kind, width, _ = w0.shape
    half = wa.shape[1]
    core = place_ref[0]
    far[pl.ds(place_ref[3] * far_count, far_count)] = f1[...]
    far[pl.ds(place_ref[4] * far_count, far_count)] = f2[...]
    low = 3 * width
    for group, (w, u) in enumerate(((w0, u0), (w1, u1), (w2, u2))):
        wall[:, group * width : (group + 1) * width, :] = w[...]
        uall[group * width : (group + 1) * width, :] = u[...]
    own_at = pl.multiple_of(low + core * half, 32)
    other_at = pl.multiple_of(low + (1 - core) * half, 32)
    wall[:, pl.ds(own_at, half), :] = wa[...]
    wall[:, pl.ds(other_at, half), :] = wb[...]
    uall[pl.ds(own_at, half), :] = ua[...]
    uall[pl.ds(other_at, half), :] = ub[...]
    inner = wall.shape[1]
    heads = inner // HD

    window = [x0[v] for v in range(var_count)] + [xs[v] for v in range(var_count)]
    window += [xo[v] for v in range(var_count)] + [far[v] for v in range(2 * far_count)]
    count = len(window)
    x_own = jnp.concatenate(window[:var_count], axis=0)
    scaled = dot_nt(x_own, wall[0]).astype(jnp.bfloat16).astype(jnp.float32) * HD ** (-0.5)
    qbuf[...] = scaled.astype(jnp.bfloat16)
    x_all = jnp.concatenate(window, axis=0)
    kbuf[...] = dot_nt(x_all, wall[1]).astype(jnp.bfloat16)
    vbuf[...] = dot_nt(x_all, wall[2]).astype(jnp.bfloat16)

    def needed(u, w):
        if w < 3 * var_count:
            return True
        w -= 3 * var_count
        if w < far_count:
            offset = u + 2 * var_count - (var_count - far_count) - w
        else:
            offset = 2 * var_count + (w - far_count) - u
        return offset <= 2 * var_count - 1

    lanes = 128
    lane = lax.broadcasted_iota(jnp.int32, (1, lanes), 1)
    lane_u = lane // heads
    sum_row = lax.broadcasted_iota(jnp.int32, (inner, lanes), 0) // HD
    sum_col = lax.broadcasted_iota(jnp.int32, (inner, lanes), 1)
    spread_row = lax.broadcasted_iota(jnp.int32, (lanes, inner), 0)
    spread_col = lax.broadcasted_iota(jnp.int32, (lanes, inner), 1) // HD
    collect = [(sum_row + u * heads == sum_col).astype(jnp.bfloat16) for u in range(var_count)]
    spread = [(spread_col + u * heads == spread_row).astype(jnp.bfloat16) for u in range(var_count)]
    own_id = jnp.full((1, lanes), -2, jnp.int32)
    for u in range(var_count):
        own_id = jnp.where(lane_u == u, ids_ref[u], own_id)
    scores = []
    for w in range(count):
        keys = kbuf[w * rows : (w + 1) * rows, :]
        score = None
        for u in range(var_count):
            if needed(u, w):
                part = jnp.dot(
                    qbuf[u * rows : (u + 1) * rows, :] * keys, collect[u], preferred_element_type=jnp.float32
                )
                score = part if score is None else score + part
        scores.append(jnp.where(own_id == ids_ref[w], score, -jnp.inf))
    highest = functools.reduce(jnp.maximum, scores)
    highest = jnp.where(lane_u < var_count, highest, 0.0)
    raised = [jnp.exp(score - highest) for score in scores]
    total = functools.reduce(lambda a, b: a + b, raised)
    share = 1.0 / jnp.where(lane_u < var_count, total, 1.0)
    for w in range(count):
        prob[w * rows : (w + 1) * rows, :] = (raised[w] * share).astype(jnp.bfloat16)
    for u in range(var_count):
        mixed = None
        for w in range(count):
            if needed(u, w):
                each = jnp.dot(
                    prob[w * rows : (w + 1) * rows, :], spread[u], preferred_element_type=jnp.float32
                )
                term = each * vbuf[w * rows : (w + 1) * rows, :].astype(jnp.float32)
                mixed = term if mixed is None else mixed + term
        att[u * rows : (u + 1) * rows, :] = mixed.astype(jnp.bfloat16)
    summed = jnp.dot(att[...], uall[...], preferred_element_type=jnp.float32)
    for u in range(var_count):
        out_ref[u] = (
            mid_ref[u].astype(jnp.float32) + summed[u * rows : (u + 1) * rows]
        ).astype(jnp.bfloat16)


def routes(var_size, patch_size):
    def route(even, odd):
        pairs = []
        for v in range(var_size):
            for p in range(patch_size):
                step = odd if v % 2 else even
                pairs.append((v * patch_size + p, v * patch_size + (p ^ step)))
        return pairs
    return route(1, 2), route(2, 1), route(3, 3)


def pairs_of(size, partner):
    return [(i, partner(i)) for i in range(size) if 0 <= partner(i) < size]


def on_device(
    tokens, patch_mask, group_ids, time_gain, time_qkv, time_out, space_gain, space_qkv, space_out
):
    var_size, patch_size = lax.axis_size("var"), lax.axis_size("patch")
    var_index, patch_index = lax.axis_index("var"), lax.axis_index("patch")
    core, level = var_index % 2, (var_index // 2) % 2
    both = ("var", "patch")
    first, second, third = routes(var_size, patch_size)
    swap = pairs_of(var_size, lambda i: i ^ 1)

    def send(block, route):
        return lax.ppermute(block, both, route)

    def partner(block):
        return lax.ppermute(block, "var", swap)

    tok = jnp.transpose(tokens, (1, 0, 2))
    mask = jnp.transpose(patch_mask)
    qkv_t = jnp.transpose(time_qkv, (1, 2, 0))
    qkv_s = jnp.transpose(space_qkv, (1, 2, 0))
    var_count, rows, depth = tok.shape
    kind, width, _ = qkv_t.shape
    half = width // 2

    tok1, tok2 = send(tok, first), send(tok, second)
    mask1, mask2, mask3 = send(mask, first), send(mask, second), send(mask, third)
    tok3 = send(tok1, second)

    def spread_weight(weight, after):
        weight, _ = lax.optimization_barrier((weight, after))
        got1 = send(weight, first)
        got2 = partner(got1)
        axis = weight.ndim - 2
        mine = lax.dynamic_slice_in_dim(got1, core * half, half, axis)
        mine = send(mine, second)
        return weight, got1, got2, mine, partner(mine)

    tout = spread_weight(time_out, (tok1, tok2))
    sqkv = spread_weight(qkv_s, (tok1, tok2))
    sout = spread_weight(space_out, (tok1, tok2))

    near, far_step = jnp.where(core == 0, 1, 2), jnp.where(core == 0, 2, 1)
    bases = jnp.stack(
        [patch_index, patch_index ^ near, patch_index ^ far_step, patch_index ^ 3]
    ).astype(jnp.int32) * rows
    marks = jnp.concatenate([mask, mask1, mask2, mask3], axis=1)
    block = jax.ShapeDtypeStruct((var_count, rows, width), jnp.bfloat16)
    att = pl.pallas_call(
        time_kernel,
        out_shape=[block] * 4,
        in_specs=[SM] + [VM] * 7,
        out_specs=[VM] * 4,
        compiler_params=params(),
        cost_estimate=cost(2_000_000_000, 4_000_000),
        name="time",
    )(bases, tok, tok1, tok2, tok3, marks, time_gain[None], qkv_t.reshape(kind * width, depth))
    att0 = att[0]
    att1, att2, att3 = send(att[1], first), send(att[2], second), send(att[3], third)

    far_count = var_count - 1
    place = jnp.stack([
        core, jnp.where(level == 0, 1, 0), jnp.where(level == 0, 0, 1),
        jnp.where(level == 0, 1, 0), jnp.where(level == 0, 0, 1),
    ]).astype(jnp.int32)
    whole = jax.ShapeDtypeStruct((var_count, rows, depth), jnp.bfloat16)
    part = jax.ShapeDtypeStruct((far_count, rows, depth), jnp.bfloat16)
    mid, x_own, far1, far2 = pl.pallas_call(
        mid_kernel,
        out_shape=[whole, whole, part, part],
        in_specs=[SM] + [VM] * 11,
        out_specs=[VM] * 4,
        scratch_shapes=[pltpu.VMEM((width, depth), jnp.bfloat16)],
        compiler_params=params(),
        cost_estimate=cost(300_000_000, 3_000_000),
        name="mid",
    )(place, att0, att1, att2, att3, *tout, tok, space_gain[None])

    x_swap = partner(x_own)
    x_other = lax.ppermute(x_own, "var", pairs_of(var_size, lambda i: i + 1 if i % 2 else i - 1))
    far1 = lax.ppermute(far1, "var", pairs_of(var_size, lambda i: i ^ 2))
    far2 = lax.ppermute(
        far2, "var", pairs_of(var_size, lambda i: i + 2 if (i // 2) % 2 else i - 2)
    )

    outside = jnp.full((2 * var_count,), -1, jnp.int32)
    padded = jnp.concatenate([outside, group_ids, outside])

    def ids_at(index, skip, size):
        return lax.dynamic_slice_in_dim(padded, (index + 2) * var_count + skip, size)

    ids = jnp.concatenate([
        ids_at(var_index, 0, var_count),
        ids_at(var_index + 1 - 2 * core, 0, var_count),
        ids_at(var_index - 1 + 2 * core, 0, var_count),
        ids_at(var_index - 2, 1, far_count),
        ids_at(var_index + 2, 0, far_count),
    ])
    inner = 4 * width
    count = 3 * var_count + 2 * far_count
    bf = jnp.bfloat16
    out = pl.pallas_call(
        space_kernel,
        out_shape=whole,
        in_specs=[SM] * 2 + [VM] * 16,
        out_specs=VM,
        scratch_shapes=[
            pltpu.VMEM((2 * far_count, rows, depth), bf),
            pltpu.VMEM((kind, inner, depth), bf),
            pltpu.VMEM((inner, depth), bf),
            pltpu.VMEM((var_count * rows, inner), bf),
            pltpu.VMEM((count * rows, inner), bf),
            pltpu.VMEM((count * rows, inner), bf),
            pltpu.VMEM((count * rows, 128), bf),
            pltpu.VMEM((var_count * rows, inner), bf),
        ],
        compiler_params=params(),
        cost_estimate=cost(4_000_000_000, 8_000_000),
        name="space",
    )(place, ids, x_own, x_swap, x_other, far1, far2, mid, *sqkv, *sout)
    return jnp.transpose(out, (1, 0, 2))


def solution(mesh):
    in_specs = (
        P("patch", ("parts", "var"), None),
        P("patch", ("parts", "var")),
        P("parts"),
        P(),
        P(None, None, "patch"),
        P("patch", None),
        P(),
        P(None, None, "patch"),
        P("patch", None),
    )
    out_specs = P("patch", ("parts", "var"), None)
    return jax.shard_map(
        on_device, mesh=mesh, in_specs=in_specs, out_specs=out_specs, check_vma=False
    )
```

```python
import functools

import jax
import jax.numpy as jnp
from jax import lax
from jax.experimental import pallas as pl
from jax.experimental.pallas import tpu as pltpu
from jax.sharding import PartitionSpec as P

HD = 64
SPACE_COST = 10_000_000_000
epsilon = 1e-06
NT = (((1,), (1,)), ((), ()))
VM = pl.BlockSpec(memory_space=pltpu.VMEM)
SM = pl.BlockSpec(memory_space=pltpu.SMEM)
HB = pl.BlockSpec(memory_space=pltpu.HBM)


def params(mib=20):
    return pltpu.CompilerParams(vmem_limit_bytes=mib * 1024 * 1024)


def cost(flops, size):
    return pl.CostEstimate(flops=flops, bytes_accessed=size, transcendentals=0)


def normed(floats, gain):
    mean = jnp.mean(floats * floats, axis=-1, keepdims=True)
    gain = gain.reshape(1, -1)
    return (floats * lax.rsqrt(mean + epsilon) * gain).astype(jnp.bfloat16)


def dot_nt(a, b):
    return lax.dot_general(a, b, NT, preferred_element_type=jnp.float32)


def project_kernel(t0, t1, t2, gain_ref, w_ref, out_ref):
    var_count, rows, depth = t0.shape
    gain = gain_ref[...]
    x = [normed(t[v].astype(jnp.float32), gain) for v in range(var_count) for t in (t0, t1, t2)]
    x = jnp.concatenate(x, axis=0)
    out_ref[...] = dot_nt(x, w_ref[...]).astype(jnp.bfloat16)


def time_kernel(
    base_ref, early_ref, t3, m0, m1, m2, m3, gain_ref, w_ref, o0, o1, o2, o3
):
    outs, masks = (o0, o1, o2, o3), (m0, m1, m2, m3)
    var_count, rows, depth = t3.shape
    width = w_ref.shape[0] // 3
    blocks = len(outs)
    total = rows * blocks
    gain = gain_ref[...]
    x = jnp.concatenate([normed(t3[v].astype(jnp.float32), gain) for v in range(var_count)], axis=0)
    late = dot_nt(x, w_ref[...]).astype(jnp.bfloat16)
    row = lax.broadcasted_iota(jnp.int32, (total, total), 0)
    col = lax.broadcasted_iota(jnp.int32, (total, total), 1)

    def positions(index):
        where = index + base_ref[0]
        for block in range(1, blocks):
            shift = base_ref[block] - block * rows
            where = jnp.where(index >= block * rows, index + shift, where)
        return where

    query_pos, key_pos = positions(row), positions(col)
    causal, same = key_pos <= query_pos, key_pos == query_pos
    head_of = lax.broadcasted_iota(jnp.int32, (1, width), 1) // HD
    marks = jnp.concatenate([m[...] for m in masks], axis=1)
    early = rows * (blocks - 1)
    for v in range(var_count):
        projected = jnp.concatenate(
            [early_ref[v * early : (v + 1) * early], late[v * rows : (v + 1) * rows]], axis=0
        )
        queries = projected[:, :width] * jnp.bfloat16(HD ** (-0.5))
        keys = projected[:, width : 2 * width]
        values = projected[:, 2 * width :]
        observed = marks[v : v + 1, :] > 0
        bias = jnp.where(causal & (observed | same), 0.0, -jnp.inf)
        attended = jnp.zeros((total, width), jnp.float32)
        for head in range(width // HD):
            mine = head_of == head
            scores = dot_nt(jnp.where(mine, queries, 0), keys) + bias
            raised = jnp.exp(scores - jnp.max(scores, axis=-1, keepdims=True))
            share = 1.0 / jnp.sum(raised, axis=-1, keepdims=True)
            weights = raised.astype(jnp.bfloat16)
            mixed = jnp.dot(weights, values, preferred_element_type=jnp.float32) * share
            attended = jnp.where(mine, mixed, attended)
        attended = attended.astype(jnp.bfloat16)
        for block, out in enumerate(outs):
            out[v] = attended[block * rows : (block + 1) * rows]


def mid_kernel(
    place_ref, a0, a1, a2, a3, w0, w1, w2, wa, wb, tok_ref, gain_ref,
    mid_ref, x_ref, f1_ref, f2_ref, last,
):
    half = wa.shape[1]
    core = place_ref[0]
    last[pl.ds(pl.multiple_of(core * half, 32), half), :] = wa[0]
    last[pl.ds(pl.multiple_of((1 - core) * half, 32), half), :] = wb[0]
    var_count, rows, depth = tok_ref.shape
    width = a0.shape[2]
    gain = gain_ref[...]
    summed = 0.0
    for a, w in ((a0, w0), (a1, w1.at[0]), (a2, w2.at[0]), (a3, last)):
        attended = a[...].reshape(var_count * rows, width)
        summed = summed + jnp.dot(attended, w[...], preferred_element_type=jnp.float32)
    mid = tok_ref[...].astype(jnp.float32).reshape(var_count * rows, depth) + summed
    mid = mid.astype(jnp.bfloat16)
    x_ref[...] = normed(mid.astype(jnp.float32), gain).reshape(tok_ref.shape)
    mid_ref[...] = mid.reshape(tok_ref.shape)
    far = f1_ref.shape[0]
    f1_ref[...] = x_ref[pl.ds(place_ref[1], far)]
    f2_ref[...] = x_ref[pl.ds(place_ref[2], far)]


def half_kernel(parts, place_ref, *refs):
    *sources, out, sems = refs
    half = out.shape[1]
    at = pl.multiple_of(place_ref[0] * half, 32)
    copies, kind = [], 0
    for source, (low, high) in zip(sources, parts):
        size = high - low
        cut = source.at[low:high, pl.ds(at, half)]
        copies.append(pltpu.make_async_copy(cut, out.at[kind : kind + size], sems.at[len(copies)]))
        copies[-1].start()
        kind += size
    for copy in copies:
        copy.wait()


def needed(u, w, var_count, far_count):
    if w < 3 * var_count:
        return True
    w -= 3 * var_count
    if w < far_count:
        offset = u + 2 * var_count - (var_count - far_count) - w
    else:
        offset = 2 * var_count + (w - far_count) - u
    return offset <= 2 * var_count - 1


def join_halves(place_ref, first, second, target, at):
    half = first.shape[0]
    core = place_ref[0]
    target[pl.ds(pl.multiple_of(at + core * half, 32), half), :] = first[...]
    target[pl.ds(pl.multiple_of(at + (1 - core) * half, 32), half), :] = second[...]


def window_kernel(place_ref, x0, xs, xo, f1, f2, xall):
    var_count, far_count = x0.shape[0], f1.shape[0]
    for block, x in enumerate((x0, xs, xo)):
        xall[block * var_count : (block + 1) * var_count] = x[...]
    xall[pl.ds(3 * var_count + place_ref[3] * far_count, far_count)] = f1[...]
    xall[pl.ds(3 * var_count + place_ref[4] * far_count, far_count)] = f2[...]


def out_kernel(place_ref, before, att, u0, u1, u2, ua, ub, mid_ref, out_ref, uall):
    width = u0.shape[0]
    for group, u in enumerate((u0, u1.at[0], u2.at[0])):
        uall[group * width : (group + 1) * width, :] = u[...]
    join_halves(place_ref, ua.at[3], ub.at[3], uall, 3 * width)
    summed, at = mid_ref[...].astype(jnp.float32).reshape(att.shape[0], -1), 0
    for attended in (before, att):
        size = attended.shape[1]
        summed = summed + jnp.dot(
            attended[...], uall[at : at + size, :], preferred_element_type=jnp.float32
        )
        at += size
    out_ref[...] = summed.astype(jnp.bfloat16).reshape(out_ref.shape)


def space_kernel(halves, var_count, place_ref, ids_ref, xall, *refs):
    *weights, out_ref, wall, qbuf, kbuf, vbuf = refs
    count, rows, depth = xall.shape
    far_count = var_count - 1
    inner = wall.shape[1]
    core = place_ref[0]
    for kind in range(3):
        if halves:
            join_halves(place_ref, weights[0].at[kind], weights[1].at[kind], wall.at[kind], 0)
        else:
            width = inner // len(weights)
            for group, weight in enumerate(weights):
                wall[kind, group * width : (group + 1) * width, :] = weight[kind]
    heads = inner // HD

    variate = place_ref[5] * var_count
    starts = (0, (1 - 2 * core) * var_count, (2 * core - 1) * var_count)
    offsets = [start + u for start in starts for u in range(var_count)]
    offsets += [u - var_count - far_count for u in range(far_count)]
    offsets += [u + 2 * var_count for u in range(far_count)]
    ids = []
    for offset in offsets:
        at = variate + offset
        inside = (at >= 0) & (at < ids_ref.shape[0])
        ids.append(jnp.where(inside, ids_ref[jnp.clip(at, 0, ids_ref.shape[0] - 1)], -1))

    scaled = dot_nt(xall[:var_count].reshape(var_count * rows, depth), wall[0]).astype(jnp.bfloat16)
    qbuf[...] = scaled * jnp.bfloat16(HD ** (-0.5))
    x_all = xall[...].reshape(count * rows, depth)
    kbuf[...] = dot_nt(x_all, wall[1]).astype(jnp.bfloat16)
    vbuf[...] = dot_nt(x_all, wall[2]).astype(jnp.bfloat16)

    lanes = 128
    lane = lax.broadcasted_iota(jnp.int32, (1, lanes), 1)
    lane_u = lane // heads
    sum_row = lax.broadcasted_iota(jnp.int32, (inner, lanes), 0) // HD
    sum_col = lax.broadcasted_iota(jnp.int32, (inner, lanes), 1)
    spread_row = lax.broadcasted_iota(jnp.int32, (lanes, inner), 0)
    spread_col = lax.broadcasted_iota(jnp.int32, (lanes, inner), 1) // HD
    collect = [(sum_row + u * heads == sum_col).astype(jnp.bfloat16) for u in range(var_count)]
    spread = [(spread_col + u * heads == spread_row).astype(jnp.bfloat16) for u in range(var_count)]
    own_id = jnp.full((1, lanes), -2, jnp.int32)
    for u in range(var_count):
        own_id = jnp.where(lane_u == u, ids[u], own_id)
    keys = kbuf[...].reshape(count, rows, inner)
    score = 0.0
    for u in range(var_count):
        product = keys * qbuf[u * rows : (u + 1) * rows, :][None]
        score = score + jnp.dot(
            product.reshape(count * rows, inner), collect[u], preferred_element_type=jnp.float32
        )
    scores = [
        jnp.where(own_id == ids[w], score[w * rows : (w + 1) * rows], -jnp.inf) for w in range(count)
    ]
    highest = functools.reduce(jnp.maximum, scores)
    highest = jnp.where(lane_u < var_count, highest, 0.0)
    raised = [jnp.exp(one - highest) for one in scores]
    total = functools.reduce(lambda a, b: a + b, raised)
    share = 1.0 / jnp.where(lane_u < var_count, total, 1.0)
    prob = jnp.concatenate([(one * share).astype(jnp.bfloat16) for one in raised], axis=0)
    for u in range(var_count):
        each = jnp.dot(prob, spread[u], preferred_element_type=jnp.float32)
        mixed = None
        for w in range(count):
            if needed(u, w, var_count, far_count):
                at = slice(w * rows, (w + 1) * rows)
                term = each[at] * vbuf[at, :].astype(jnp.float32)
                mixed = term if mixed is None else mixed + term
        out_ref[u * rows : (u + 1) * rows, :] = mixed.astype(jnp.bfloat16)


def routes(var_size, patch_size):
    def route(even, odd):
        pairs = []
        for v in range(var_size):
            for p in range(patch_size):
                step = odd if v % 2 else even
                pairs.append((v * patch_size + p, v * patch_size + (p ^ step)))
        return pairs
    return route(1, 2), route(2, 1), route(3, 3)


def tied(blocks, after):
    return lax.optimization_barrier((*blocks, after))


def pairs_of(size, partner):
    return [(i, partner(i)) for i in range(size) if 0 <= partner(i) < size]


def on_device(
    tokens, patch_mask, group_ids, time_gain, time_qkv, time_out, space_gain, space_qkv, space_out
):
    var_size, patch_size = lax.axis_size("var"), lax.axis_size("patch")
    var_index, patch_index = lax.axis_index("var"), lax.axis_index("patch")
    core, level = var_index % 2, (var_index // 2) % 2
    both = ("var", "patch")
    first, second, third = routes(var_size, patch_size)
    swap = pairs_of(var_size, lambda i: i ^ 1)

    def send(block, route):
        return lax.ppermute(block, both, route)

    def partner(block):
        return lax.ppermute(block, "var", swap)

    tok = jnp.transpose(tokens, (1, 0, 2))
    mask = jnp.transpose(patch_mask)
    qkv_t = jnp.transpose(time_qkv, (1, 2, 0))
    qkv_s = jnp.transpose(space_qkv, (1, 2, 0))
    var_count, rows, depth = tok.shape
    kind, width, _ = qkv_t.shape
    half = width // 2

    tok1, tok2 = send(tok, first), send(tok, second)
    mask1, mask2, mask3 = send(mask, first), send(mask, second), send(mask, third)
    tok1f, mask1, mask2, mask3 = lax.optimization_barrier((tok1, mask1, mask2, mask3))
    tok3 = send(tok1f, second)
    weight = qkv_t.reshape(kind * width, depth)
    bf = jnp.bfloat16
    early = pl.pallas_call(
        project_kernel,
        out_shape=jax.ShapeDtypeStruct((3 * var_count * rows, kind * width), bf),
        in_specs=[VM] * 5,
        out_specs=VM,
        compiler_params=params(),
        cost_estimate=cost(1000, 1000),
        name="project",
    )(tok, tok1f, tok2, time_gain, weight)

    def half_of(parts, *blocks, weight=1000):
        return pl.pallas_call(
            functools.partial(half_kernel, parts),
            out_shape=jax.ShapeDtypeStruct((sum(b - a for a, b in parts), half, depth), bf),
            in_specs=[SM] + [HB] * len(blocks),
            out_specs=HB,
            scratch_shapes=[pltpu.SemaphoreType.DMA((len(blocks),))],
            compiler_params=params(1),
            cost_estimate=cost(weight, 1000),
            name="half",
        )(place, *blocks)

    far_count = var_count - 1
    place = jnp.stack([
        core, jnp.where(level == 0, 1, 0), jnp.where(level == 0, 0, 1),
        jnp.where(level == 0, 1, 0), jnp.where(level == 0, 0, 1), var_index,
    ]).astype(jnp.int32)
    t_half = half_of(((0, 1),), time_out[None])
    t_own, t_half, early = lax.optimization_barrier((time_out[None], t_half, early))
    t1, ta = send(t_own, first), send(t_half, third)

    near, far_step = jnp.where(core == 0, 1, 2), jnp.where(core == 0, 2, 1)
    bases = jnp.stack(
        [patch_index, patch_index ^ near, patch_index ^ far_step, patch_index ^ 3]
    ).astype(jnp.int32) * rows
    block = jax.ShapeDtypeStruct((var_count, rows, width), bf)
    att = pl.pallas_call(
        time_kernel,
        out_shape=[block] * 4,
        in_specs=[SM] + [VM] * 8,
        out_specs=[VM] * 4,
        compiler_params=params(),
        cost_estimate=cost(1000, 1000),
        name="time",
    )(bases, early, tok3, mask, mask1, mask2, mask3, time_gain, weight)
    att0 = att[0]
    att1, att3, att2 = send(att[1], first), send(att[3], third), send(att[2], second)
    s_qkv, s_out, t1, ta, att1, att2, att3 = lax.optimization_barrier(
        (qkv_s, space_out[None], t1, ta, att1, att2, att3)
    )
    t2, tb = partner(t1), partner(ta)
    qkv1, u1 = send(s_qkv, first), send(s_out, first)

    whole = jax.ShapeDtypeStruct((var_count, rows, depth), jnp.bfloat16)
    part = jax.ShapeDtypeStruct((far_count, rows, depth), jnp.bfloat16)
    mid, x_own, far1, far2 = pl.pallas_call(
        mid_kernel,
        out_shape=[whole, whole, part, part],
        in_specs=[SM] + [VM] * 11,
        out_specs=[VM] * 4,
        scratch_shapes=[pltpu.VMEM((width, depth), bf)],
        compiler_params=params(),
        cost_estimate=cost(1000, 1000),
        name="mid",
    )(place, att0, att1, att2, att3, time_out, t1, t2, ta, tb, tok, space_gain)

    x_other = lax.ppermute(x_own, "var", pairs_of(var_size, lambda i: i + 1 if i % 2 else i - 1))
    x_swap = partner(x_own)
    far1 = lax.ppermute(far1, "var", pairs_of(var_size, lambda i: i ^ 2))
    far2 = lax.ppermute(
        far2, "var", pairs_of(var_size, lambda i: i + 2 if (i // 2) % 2 else i - 2)
    )
    count = 3 * var_count + 2 * far_count
    own_rows = var_count * rows
    window = pl.pallas_call(
        window_kernel,
        out_shape=jax.ShapeDtypeStruct((count, rows, depth), bf),
        in_specs=[SM] + [VM] * 5,
        out_specs=VM,
        compiler_params=params(8),
        cost_estimate=cost(1000, 1000),
        name="window",
    )(place, x_own, x_swap, x_other, far1, far2)
    qkv1, u1, window = lax.optimization_barrier((qkv1, u1, window))
    rest_a = send(half_of(((0, 3), (0, 1)), qkv1, u1), second)
    qkv2 = partner(qkv1)

    def attend(groups, *weights):
        inner = width * groups
        return pl.pallas_call(
            functools.partial(space_kernel, groups == 1, var_count),
            out_shape=jax.ShapeDtypeStruct((own_rows, inner), bf),
            in_specs=[SM] * 2 + [VM] * (1 + len(weights)),
            out_specs=VM,
            scratch_shapes=[
                pltpu.VMEM((kind, inner, depth), bf),
                pltpu.VMEM((own_rows, inner), bf),
                pltpu.VMEM((count * rows, inner), bf),
                pltpu.VMEM((count * rows, inner), bf),
            ],
            compiler_params=params(),
            cost_estimate=cost(1000 if groups == 1 else SPACE_COST, 1000),
            name="space_last" if groups == 1 else "space",
        )(place, group_ids, window, *weights)

    first_parts = attend(3, qkv_s, qkv1, qkv2)
    rest_a, u1, first_parts = lax.optimization_barrier((rest_a, u1, first_parts))
    rest_b, u2 = partner(rest_a), partner(u1)
    last_part = attend(1, rest_a, rest_b)
    out = pl.pallas_call(
        out_kernel,
        out_shape=whole,
        in_specs=[SM] + [VM] * 8,
        out_specs=VM,
        scratch_shapes=[pltpu.VMEM((4 * width, depth), bf)],
        compiler_params=params(),
        cost_estimate=cost(1000, 1000),
        name="out",
    )(place, first_parts, last_part, space_out, u1, u2, rest_a, rest_b, mid)
    return jnp.transpose(out, (1, 0, 2))


def solution(mesh):
    in_specs = (
        P("patch", ("parts", "var"), None),
        P("patch", ("parts", "var")),
        P("parts"),
        P(),
        P(None, None, "patch"),
        P("patch", None),
        P(),
        P(None, None, "patch"),
        P("patch", None),
    )
    out_specs = P("patch", ("parts", "var"), None)
    return jax.shard_map(
        on_device, mesh=mesh, in_specs=in_specs, out_specs=out_specs, check_vma=False
    )
```

```python
import functools

import jax
import jax.numpy as jnp
from jax import lax
from jax.experimental import pallas as pl
from jax.experimental.pallas import tpu as pltpu
from jax.sharding import PartitionSpec as P

HD = 64
SPACE_COST = 10_000_000_000
epsilon = 1e-06
NT = (((1,), (1,)), ((), ()))
VM = pl.BlockSpec(memory_space=pltpu.VMEM)
SM = pl.BlockSpec(memory_space=pltpu.SMEM)
HB = pl.BlockSpec(memory_space=pltpu.HBM)


def params(mib=20):
    return pltpu.CompilerParams(vmem_limit_bytes=mib * 1024 * 1024)


def cost(flops, size):
    return pl.CostEstimate(flops=flops, bytes_accessed=size, transcendentals=0)


def normed(floats, gain):
    mean = jnp.mean(floats * floats, axis=-1, keepdims=True)
    gain = gain.reshape(1, -1)
    return (floats * lax.rsqrt(mean + epsilon) * gain).astype(jnp.bfloat16)


def dot_nt(a, b):
    return lax.dot_general(a, b, NT, preferred_element_type=jnp.float32)


def project_kernel(t0, t1, t2, gain_ref, w_ref, out_ref):
    var_count, rows, depth = t0.shape
    gain = gain_ref[...]
    x = [normed(t[v].astype(jnp.float32), gain) for v in range(var_count) for t in (t0, t1, t2)]
    x = jnp.concatenate(x, axis=0)
    out_ref[...] = dot_nt(x, w_ref[...]).astype(jnp.bfloat16)


def time_kernel(
    base_ref, early_ref, t3, m0, m1, m2, m3, gain_ref, w_ref, o0, o2, o13
):
    masks = (m0, m1, m2, m3)
    var_count, rows, depth = t3.shape
    width = w_ref.shape[0] // 3
    blocks = len(masks)
    total = rows * blocks
    gain = gain_ref[...]
    x = jnp.concatenate([normed(t3[v].astype(jnp.float32), gain) for v in range(var_count)], axis=0)
    late = dot_nt(x, w_ref[...]).astype(jnp.bfloat16)
    row = lax.broadcasted_iota(jnp.int32, (total, total), 0)
    col = lax.broadcasted_iota(jnp.int32, (total, total), 1)

    def positions(index):
        where = index + base_ref[0]
        for block in range(1, blocks):
            shift = base_ref[block] - block * rows
            where = jnp.where(index >= block * rows, index + shift, where)
        return where

    query_pos, key_pos = positions(row), positions(col)
    causal, same = key_pos <= query_pos, key_pos == query_pos
    head_of = lax.broadcasted_iota(jnp.int32, (1, width), 1) // HD
    marks = jnp.concatenate([m[...] for m in masks], axis=1)
    early = rows * (blocks - 1)
    for v in range(var_count):
        projected = jnp.concatenate(
            [early_ref[v * early : (v + 1) * early], late[v * rows : (v + 1) * rows]], axis=0
        )
        queries = projected[:, :width] * jnp.bfloat16(HD ** (-0.5))
        keys = projected[:, width : 2 * width]
        values = projected[:, 2 * width :]
        observed = marks[v : v + 1, :] > 0
        bias = jnp.where(causal & (observed | same), 0.0, -jnp.inf)
        attended = jnp.zeros((total, width), jnp.float32)
        for head in range(width // HD):
            mine = head_of == head
            scores = dot_nt(jnp.where(mine, queries, 0), keys) + bias
            raised = jnp.exp(scores - jnp.max(scores, axis=-1, keepdims=True))
            share = 1.0 / jnp.sum(raised, axis=-1, keepdims=True)
            weights = raised.astype(jnp.bfloat16)
            mixed = jnp.dot(weights, values, preferred_element_type=jnp.float32) * share
            attended = jnp.where(mine, mixed, attended)
        attended = attended.astype(jnp.bfloat16)
        places = (o0.at[v], o13.at[v], o2.at[v], o13.at[var_count + v])
        for block, out in enumerate(places):
            out[...] = attended[block * rows : (block + 1) * rows]


def part_kernel(a2, got, w0, w1, out_ref):
    var_count, rows, width = a2.shape
    own = a2[...].reshape(var_count * rows, width)
    other = got[var_count:].reshape(var_count * rows, width)
    summed = jnp.dot(own, w0[...], preferred_element_type=jnp.float32)
    summed = summed + jnp.dot(other, w1[0], preferred_element_type=jnp.float32)
    out_ref[...] = summed.astype(jnp.bfloat16).reshape(out_ref.shape)


def mid_kernel(
    place_ref, a0, got, w0, w1, part_ref, tok_ref, gain_ref, mid_ref, x_ref
):
    var_count, rows, depth = tok_ref.shape
    width = a0.shape[2]
    gain = gain_ref[...]
    own = a0[...].reshape(var_count * rows, width)
    other = got[:var_count].reshape(var_count * rows, width)
    summed = part_ref[...].astype(jnp.float32).reshape(var_count * rows, depth)
    summed = summed + jnp.dot(own, w0[...], preferred_element_type=jnp.float32)
    summed = summed + jnp.dot(other, w1[0], preferred_element_type=jnp.float32)
    mid = tok_ref[...].astype(jnp.float32).reshape(var_count * rows, depth) + summed
    mid = mid.astype(jnp.bfloat16)
    x_ref[...] = normed(mid.astype(jnp.float32), gain).reshape(tok_ref.shape)
    mid_ref[...] = mid.reshape(tok_ref.shape)


def half_kernel(parts, place_ref, *refs):
    *sources, out, sems = refs
    half = out.shape[1]
    at = pl.multiple_of(place_ref[0] * half, 32)
    copies, kind = [], 0
    for source, (low, high) in zip(sources, parts):
        size = high - low
        cut = source.at[low:high, pl.ds(at, half)]
        copies.append(pltpu.make_async_copy(cut, out.at[kind : kind + size], sems.at[len(copies)]))
        copies[-1].start()
        kind += size
    for copy in copies:
        copy.wait()


def needed(u, w, var_count, far_count):
    if w < 3 * var_count:
        return True
    w -= 3 * var_count
    if w < far_count:
        offset = u + 2 * var_count - (var_count - far_count) - w
    else:
        offset = 2 * var_count + (w - far_count) - u
    return offset <= 2 * var_count - 1


def join_halves(place_ref, first, second, target, at):
    half = first.shape[0]
    core = place_ref[0]
    target[pl.ds(pl.multiple_of(at + core * half, 32), half), :] = first[...]
    target[pl.ds(pl.multiple_of(at + (1 - core) * half, 32), half), :] = second[...]


def window_kernel(place_ref, x0, xs, got1, got2, swapped1, swapped2, xall):
    var_count = x0.shape[0]
    core, up_first = place_ref[0], place_ref[1] == 1
    xall[:var_count] = x0[...]
    xall[var_count : 2 * var_count] = xs[...]
    other_first = up_first == (core == 1)
    xall[2 * var_count : 3 * var_count] = jnp.where(other_first, swapped1[...], swapped2[...])
    at = 3 * var_count
    xall[at : at + var_count - 1] = jnp.where(up_first, got2[1:], got1[1:])
    at += var_count - 1
    xall[at : at + var_count - 1] = jnp.where(up_first, got1[:-1], got2[:-1])


def out_kernel(place_ref, before, att, u0, u1, u2, ua, ub, mid_ref, out_ref, uall):
    width = u0.shape[0]
    for group, u in enumerate((u0, u1.at[0], u2.at[0])):
        uall[group * width : (group + 1) * width, :] = u[...]
    join_halves(place_ref, ua.at[3], ub.at[3], uall, 3 * width)
    summed, at = mid_ref[...].astype(jnp.float32).reshape(att.shape[0], -1), 0
    for attended in (before, att):
        size = attended.shape[1]
        summed = summed + jnp.dot(
            attended[...], uall[at : at + size, :], preferred_element_type=jnp.float32
        )
        at += size
    out_ref[...] = summed.astype(jnp.bfloat16).reshape(out_ref.shape)


def space_kernel(halves, var_count, place_ref, ids_ref, xall, *refs):
    *weights, out_ref, wall, qbuf, kbuf, vbuf = refs
    count, rows, depth = xall.shape
    far_count = var_count - 1
    inner = wall.shape[1]
    core = place_ref[0]
    for kind in range(3):
        if halves:
            join_halves(place_ref, weights[0].at[kind], weights[1].at[kind], wall.at[kind], 0)
        else:
            width = inner // len(weights)
            for group, weight in enumerate(weights):
                wall[kind, group * width : (group + 1) * width, :] = weight[kind]
    heads = inner // HD

    variate = place_ref[2] * var_count
    starts = (0, (1 - 2 * core) * var_count, (2 * core - 1) * var_count)
    offsets = [start + u for start in starts for u in range(var_count)]
    offsets += [u - var_count - far_count for u in range(far_count)]
    offsets += [u + 2 * var_count for u in range(far_count)]
    ids = []
    for offset in offsets:
        at = variate + offset
        inside = (at >= 0) & (at < ids_ref.shape[0])
        ids.append(jnp.where(inside, ids_ref[jnp.clip(at, 0, ids_ref.shape[0] - 1)], -1))

    scaled = dot_nt(xall[:var_count].reshape(var_count * rows, depth), wall[0]).astype(jnp.bfloat16)
    qbuf[...] = scaled * jnp.bfloat16(HD ** (-0.5))
    x_all = xall[...].reshape(count * rows, depth)
    kbuf[...] = dot_nt(x_all, wall[1]).astype(jnp.bfloat16)
    vbuf[...] = dot_nt(x_all, wall[2]).astype(jnp.bfloat16)

    lanes = 128
    lane = lax.broadcasted_iota(jnp.int32, (1, lanes), 1)
    lane_u = lane // heads
    sum_row = lax.broadcasted_iota(jnp.int32, (inner, lanes), 0) // HD
    sum_col = lax.broadcasted_iota(jnp.int32, (inner, lanes), 1)
    spread_row = lax.broadcasted_iota(jnp.int32, (lanes, inner), 0)
    spread_col = lax.broadcasted_iota(jnp.int32, (lanes, inner), 1) // HD
    collect = [(sum_row + u * heads == sum_col).astype(jnp.bfloat16) for u in range(var_count)]
    spread = [(spread_col + u * heads == spread_row).astype(jnp.bfloat16) for u in range(var_count)]
    own_id = jnp.full((1, lanes), -2, jnp.int32)
    for u in range(var_count):
        own_id = jnp.where(lane_u == u, ids[u], own_id)
    keys = kbuf[...].reshape(count, rows, inner)
    score = 0.0
    for u in range(var_count):
        product = keys * qbuf[u * rows : (u + 1) * rows, :][None]
        score = score + jnp.dot(
            product.reshape(count * rows, inner), collect[u], preferred_element_type=jnp.float32
        )
    scores = [
        jnp.where(own_id == ids[w], score[w * rows : (w + 1) * rows], -jnp.inf) for w in range(count)
    ]
    highest = functools.reduce(jnp.maximum, scores)
    highest = jnp.where(lane_u < var_count, highest, 0.0)
    raised = [jnp.exp(one - highest) for one in scores]
    total = functools.reduce(lambda a, b: a + b, raised)
    share = 1.0 / jnp.where(lane_u < var_count, total, 1.0)
    prob = jnp.concatenate([(one * share).astype(jnp.bfloat16) for one in raised], axis=0)
    for u in range(var_count):
        each = jnp.dot(prob, spread[u], preferred_element_type=jnp.float32)
        mixed = None
        for w in range(count):
            if needed(u, w, var_count, far_count):
                at = slice(w * rows, (w + 1) * rows)
                term = each[at] * vbuf[at, :].astype(jnp.float32)
                mixed = term if mixed is None else mixed + term
        out_ref[u * rows : (u + 1) * rows, :] = mixed.astype(jnp.bfloat16)


def routes(var_size, patch_size):
    def route(even, odd):
        pairs = []
        for v in range(var_size):
            for p in range(patch_size):
                step = odd if v % 2 else even
                pairs.append((v * patch_size + p, v * patch_size + (p ^ step)))
        return pairs
    return route(1, 2), route(2, 1), route(3, 3)


def tied(blocks, after):
    return lax.optimization_barrier((*blocks, after))


def pairs_of(size, partner):
    return [(i, partner(i)) for i in range(size) if 0 <= partner(i) < size]


def on_device(
    tokens, patch_mask, group_ids, time_gain, time_qkv, time_out, space_gain, space_qkv, space_out
):
    var_size, patch_size = lax.axis_size("var"), lax.axis_size("patch")
    var_index, patch_index = lax.axis_index("var"), lax.axis_index("patch")
    core = var_index % 2
    both = ("var", "patch")
    first, second, third = routes(var_size, patch_size)
    swap = pairs_of(var_size, lambda i: i ^ 1)

    def send(block, route):
        return lax.ppermute(block, both, route)

    def partner(block):
        return lax.ppermute(block, "var", swap)

    tok = jnp.transpose(tokens, (1, 0, 2))
    mask = jnp.transpose(patch_mask)
    qkv_t = jnp.transpose(time_qkv, (1, 2, 0))
    qkv_s = jnp.transpose(space_qkv, (1, 2, 0))
    var_count, rows, depth = tok.shape
    kind, width, _ = qkv_t.shape
    half = width // 2

    tok1, tok2 = send(tok, first), send(tok, second)
    mask1, mask2, mask3 = send(mask, first), send(mask, second), send(mask, third)
    tok1f, mask1, mask2, mask3 = lax.optimization_barrier((tok1, mask1, mask2, mask3))
    tok3 = send(tok1f, second)
    weight = qkv_t.reshape(kind * width, depth)
    bf = jnp.bfloat16
    early = pl.pallas_call(
        project_kernel,
        out_shape=jax.ShapeDtypeStruct((3 * var_count * rows, kind * width), bf),
        in_specs=[VM] * 5,
        out_specs=VM,
        compiler_params=params(),
        cost_estimate=cost(1000, 1000),
        name="project",
    )(tok, tok1f, tok2, time_gain, weight)

    def half_of(parts, *blocks, weight=1000):
        return pl.pallas_call(
            functools.partial(half_kernel, parts),
            out_shape=jax.ShapeDtypeStruct((sum(b - a for a, b in parts), half, depth), bf),
            in_specs=[SM] + [HB] * len(blocks),
            out_specs=HB,
            scratch_shapes=[pltpu.SemaphoreType.DMA((len(blocks),))],
            compiler_params=params(1),
            cost_estimate=cost(weight, 1000),
            name="half",
        )(place, *blocks)

    far_count = var_count - 1
    level = (var_index // 2) % 2
    place = jnp.stack([core, 1 - level, var_index]).astype(jnp.int32)
    t_own, early = lax.optimization_barrier((time_out[None], early))
    t1 = send(t_own, first)

    near, far_step = jnp.where(core == 0, 1, 2), jnp.where(core == 0, 2, 1)
    bases = jnp.stack(
        [patch_index, patch_index ^ near, patch_index ^ far_step, patch_index ^ 3]
    ).astype(jnp.int32) * rows
    block = jax.ShapeDtypeStruct((var_count, rows, width), bf)
    att = pl.pallas_call(
        time_kernel,
        out_shape=[block, block, jax.ShapeDtypeStruct((2 * var_count, rows, width), bf)],
        in_specs=[SM] + [VM] * 8,
        out_specs=[VM] * 3,
        compiler_params=params(),
        cost_estimate=cost(10_000_000_000, 1000),
        name="time",
    )(bases, early, tok3, mask, mask1, mask2, mask3, time_gain, weight)
    att0, att2, att13 = att
    got = send(att13, first)
    s_qkv, s_out, got = lax.optimization_barrier((qkv_s, space_out[None], got))
    whole = jax.ShapeDtypeStruct((var_count, rows, depth), jnp.bfloat16)
    part = jax.ShapeDtypeStruct((far_count, rows, depth), jnp.bfloat16)
    partial = pl.pallas_call(
        part_kernel,
        out_shape=whole,
        in_specs=[VM] * 4,
        out_specs=VM,
        compiler_params=params(),
        cost_estimate=cost(1000, 1000),
        name="part",
    )(att2, got, time_out, t1)
    partial = send(partial, second)
    qkv1, u1 = send(s_qkv, first), send(s_out, first)
    mid, x_own = pl.pallas_call(
        mid_kernel,
        out_shape=[whole, whole],
        in_specs=[SM] + [VM] * 7,
        out_specs=[VM] * 2,
        compiler_params=params(),
        cost_estimate=cost(1000, 1000),
        name="mid",
    )(place, att0, got, time_out, t1, partial, tok, space_gain)

    got1 = lax.ppermute(x_own, "var", pairs_of(var_size, lambda i: i ^ 2))
    got2 = lax.ppermute(
        x_own, "var", pairs_of(var_size, lambda i: i + 2 if (i // 2) % 2 else i - 2)
    )
    x_swap = partner(x_own)
    qkv1, u1, x_swap = lax.optimization_barrier((qkv1, u1, x_swap))
    rest_a = send(half_of(((0, 3), (0, 1)), qkv1, u1), second)
    swapped1, swapped2 = partner(got1), partner(got2)
    count = 3 * var_count + 2 * far_count
    own_rows = var_count * rows
    window = pl.pallas_call(
        window_kernel,
        out_shape=jax.ShapeDtypeStruct((count, rows, depth), bf),
        in_specs=[SM] + [VM] * 6,
        out_specs=VM,
        compiler_params=params(8),
        cost_estimate=cost(1000, 1000),
        name="window",
    )(place, x_own, x_swap, got1, got2, swapped1, swapped2)
    qkv1, window = lax.optimization_barrier((qkv1, window))
    qkv2 = partner(qkv1)

    def attend(groups, *weights):
        inner = width * groups
        return pl.pallas_call(
            functools.partial(space_kernel, groups == 1, var_count),
            out_shape=jax.ShapeDtypeStruct((own_rows, inner), bf),
            in_specs=[SM] * 2 + [VM] * (1 + len(weights)),
            out_specs=VM,
            scratch_shapes=[
                pltpu.VMEM((kind, inner, depth), bf),
                pltpu.VMEM((own_rows, inner), bf),
                pltpu.VMEM((count * rows, inner), bf),
                pltpu.VMEM((count * rows, inner), bf),
            ],
            compiler_params=params(),
            cost_estimate=cost(1000 if groups == 1 else SPACE_COST, 1000),
            name="space_last" if groups == 1 else "space",
        )(place, group_ids, window, *weights)

    first_parts = attend(3, qkv_s, qkv1, qkv2)
    rest_a, u1, first_parts = lax.optimization_barrier((rest_a, u1, first_parts))
    rest_b, u2 = partner(rest_a), partner(u1)
    last_part = attend(1, rest_a, rest_b)
    out = pl.pallas_call(
        out_kernel,
        out_shape=whole,
        in_specs=[SM] + [VM] * 8,
        out_specs=VM,
        scratch_shapes=[pltpu.VMEM((4 * width, depth), bf)],
        compiler_params=params(),
        cost_estimate=cost(1000, 1000),
        name="out",
    )(place, first_parts, last_part, space_out, u1, u2, rest_a, rest_b, mid)
    return jnp.transpose(out, (1, 0, 2))


def solution(mesh):
    in_specs = (
        P("patch", ("parts", "var"), None),
        P("patch", ("parts", "var")),
        P("parts"),
        P(),
        P(None, None, "patch"),
        P("patch", None),
        P(),
        P(None, None, "patch"),
        P("patch", None),
    )
    out_specs = P("patch", ("parts", "var"), None)
    return jax.shard_map(
        on_device, mesh=mesh, in_specs=in_specs, out_specs=out_specs, check_vma=False
    )
```

```python
import functools

import jax
import jax.numpy as jnp
from jax import lax
from jax.experimental import pallas as pl
from jax.experimental.pallas import tpu as pltpu
from jax.sharding import PartitionSpec as P

HD = 64
SPACE_COST = 10_000_000_000
epsilon = 1e-06
NT = (((1,), (1,)), ((), ()))
VM = pl.BlockSpec(memory_space=pltpu.VMEM)
SM = pl.BlockSpec(memory_space=pltpu.SMEM)
HB = pl.BlockSpec(memory_space=pltpu.HBM)


def params(mib=20):
    return pltpu.CompilerParams(vmem_limit_bytes=mib * 1024 * 1024)


def cost(flops, size):
    return pl.CostEstimate(flops=flops, bytes_accessed=size, transcendentals=0)


def normed(floats, gain):
    mean = jnp.mean(floats * floats, axis=-1, keepdims=True)
    gain = gain.reshape(1, -1)
    return (floats * lax.rsqrt(mean + epsilon) * gain).astype(jnp.bfloat16)


def dot_nt(a, b):
    return lax.dot_general(a, b, NT, preferred_element_type=jnp.float32)


def project_kernel(t0, t1, t2, gain_ref, w_ref, out_ref):
    var_count, rows, depth = t0.shape
    gain = gain_ref[...]
    x = [normed(t[v].astype(jnp.float32), gain) for v in range(var_count) for t in (t0, t1, t2)]
    x = jnp.concatenate(x, axis=0)
    out_ref[...] = dot_nt(x, w_ref[...]).astype(jnp.bfloat16)


def time_kernel(
    base_ref, early_ref, t3, m0, m1, m2, m3, gain_ref, w_ref, o0, o2, o13
):
    masks = (m0, m1, m2, m3)
    var_count, rows, depth = t3.shape
    width = w_ref.shape[0] // 3
    blocks = len(masks)
    total = rows * blocks
    gain = gain_ref[...]
    x = jnp.concatenate([normed(t3[v].astype(jnp.float32), gain) for v in range(var_count)], axis=0)
    late = dot_nt(x, w_ref[...]).astype(jnp.bfloat16)
    row = lax.broadcasted_iota(jnp.int32, (total, total), 0)
    col = lax.broadcasted_iota(jnp.int32, (total, total), 1)

    def positions(index):
        where = index + base_ref[0]
        for block in range(1, blocks):
            shift = base_ref[block] - block * rows
            where = jnp.where(index >= block * rows, index + shift, where)
        return where

    query_pos, key_pos = positions(row), positions(col)
    causal, same = key_pos <= query_pos, key_pos == query_pos
    head_of = lax.broadcasted_iota(jnp.int32, (1, width), 1) // HD
    marks = jnp.concatenate([m[...] for m in masks], axis=1)
    early = rows * (blocks - 1)
    for v in range(var_count):
        projected = jnp.concatenate(
            [early_ref[v * early : (v + 1) * early], late[v * rows : (v + 1) * rows]], axis=0
        )
        queries = projected[:, :width] * jnp.bfloat16(HD ** (-0.5))
        keys = projected[:, width : 2 * width]
        values = projected[:, 2 * width :]
        observed = marks[v : v + 1, :] > 0
        bias = jnp.where(causal & (observed | same), 0.0, -jnp.inf)
        attended = jnp.zeros((total, width), jnp.float32)
        for head in range(width // HD):
            mine = head_of == head
            scores = dot_nt(jnp.where(mine, queries, 0), keys) + bias
            raised = jnp.exp(scores - jnp.max(scores, axis=-1, keepdims=True))
            share = 1.0 / jnp.sum(raised, axis=-1, keepdims=True)
            weights = raised.astype(jnp.bfloat16)
            mixed = jnp.dot(weights, values, preferred_element_type=jnp.float32) * share
            attended = jnp.where(mine, mixed, attended)
        attended = attended.astype(jnp.bfloat16)
        places = (o0.at[v], o13.at[v], o2.at[v], o13.at[var_count + v])
        for block, out in enumerate(places):
            out[...] = attended[block * rows : (block + 1) * rows]


def part_kernel(a2, got, w0, w1, out_ref):
    var_count, rows, width = a2.shape
    own = a2[...].reshape(var_count * rows, width)
    other = got[var_count:].reshape(var_count * rows, width)
    summed = jnp.dot(own, w0[...], preferred_element_type=jnp.float32)
    summed = summed + jnp.dot(other, w1[0], preferred_element_type=jnp.float32)
    out_ref[...] = summed.astype(jnp.bfloat16).reshape(out_ref.shape)


def mid_kernel(
    place_ref, a0, got, w0, w1, part_ref, tok_ref, gain_ref, mid_ref, x_ref
):
    var_count, rows, depth = tok_ref.shape
    width = a0.shape[2]
    gain = gain_ref[...]
    own = a0[...].reshape(var_count * rows, width)
    other = got[:var_count].reshape(var_count * rows, width)
    summed = part_ref[...].astype(jnp.float32).reshape(var_count * rows, depth)
    summed = summed + jnp.dot(own, w0[...], preferred_element_type=jnp.float32)
    summed = summed + jnp.dot(other, w1[0], preferred_element_type=jnp.float32)
    mid = tok_ref[...].astype(jnp.float32).reshape(var_count * rows, depth) + summed
    mid = mid.astype(jnp.bfloat16)
    x_ref[...] = normed(mid.astype(jnp.float32), gain).reshape(tok_ref.shape)
    mid_ref[...] = mid.reshape(tok_ref.shape)


def split_kernel(place_ref, qkv_hbm, u_hbm, mine_hbm, other_hbm, sems):
    kinds, half, core = qkv_hbm.shape[0], mine_hbm.shape[1], place_ref[0]
    copies = []
    for target, index in ((mine_hbm, core), (other_hbm, 1 - core)):
        at = pl.multiple_of(index * half, 32)
        for source, part in (
            (qkv_hbm.at[:, pl.ds(at, half)], target.at[:kinds]),
            (u_hbm.at[pl.ds(at, half)], target.at[kinds]),
        ):
            copies.append(pltpu.make_async_copy(source, part, sems.at[len(copies)]))
            copies[-1].start()
    for copy in copies:
        copy.wait()


def needed(u, w, var_count, far_count):
    if w < 3 * var_count:
        return True
    w -= 3 * var_count
    if w < far_count:
        offset = u + 2 * var_count - (var_count - far_count) - w
    else:
        offset = 2 * var_count + (w - far_count) - u
    return offset <= 2 * var_count - 1


def join_halves(place_ref, first, second, target, at):
    half = first.shape[0]
    core = place_ref[0]
    target[pl.ds(pl.multiple_of(at + core * half, 32), half), :] = first[...]
    target[pl.ds(pl.multiple_of(at + (1 - core) * half, 32), half), :] = second[...]


def window_kernel(place_ref, x0, xs, got1, got2, swapped1, swapped2, xall):
    var_count = x0.shape[0]
    core, up_first = place_ref[0], place_ref[1] == 1
    xall[:var_count] = x0[...]
    xall[var_count : 2 * var_count] = xs[...]
    other_first = up_first == (core == 1)
    xall[2 * var_count : 3 * var_count] = jnp.where(other_first, swapped1[...], swapped2[...])
    at = 3 * var_count
    xall[at : at + var_count - 1] = jnp.where(up_first, got2[1:], got1[1:])
    at += var_count - 1
    xall[at : at + var_count - 1] = jnp.where(up_first, got1[:-1], got2[:-1])


def space_kernel(
    var_count, place_ref, ids_ref, xall, own, u_own, c1, o1, c2, o2, c3, o3, mid_ref,
    out_ref, wall, uall, qbuf, kbuf, vbuf, att,
):
    count, rows, depth = xall.shape
    far_count = var_count - 1
    inner = wall.shape[1]
    core = place_ref[0]
    width = u_own.shape[0]
    for kind in range(4):
        target = wall.at[kind] if kind < 3 else uall
        target[:width, :] = own[kind] if kind < 3 else u_own[...]
        join_halves(place_ref, c1.at[kind], o1.at[kind], target, width)
        join_halves(place_ref, o2.at[kind], c2.at[kind], target, 2 * width)
        join_halves(place_ref, c3.at[kind], o3.at[kind], target, 3 * width)
    heads = inner // HD

    variate = place_ref[2] * var_count
    starts = (0, (1 - 2 * core) * var_count, (2 * core - 1) * var_count)
    offsets = [start + u for start in starts for u in range(var_count)]
    offsets += [u - var_count - far_count for u in range(far_count)]
    offsets += [u + 2 * var_count for u in range(far_count)]
    ids = []
    for offset in offsets:
        at = variate + offset
        inside = (at >= 0) & (at < ids_ref.shape[0])
        ids.append(jnp.where(inside, ids_ref[jnp.clip(at, 0, ids_ref.shape[0] - 1)], -1))

    scaled = dot_nt(xall[:var_count].reshape(var_count * rows, depth), wall[0]).astype(jnp.bfloat16)
    qbuf[...] = scaled * jnp.bfloat16(HD ** (-0.5))
    x_all = xall[...].reshape(count * rows, depth)
    kbuf[...] = dot_nt(x_all, wall[1]).astype(jnp.bfloat16)
    vbuf[...] = dot_nt(x_all, wall[2]).astype(jnp.bfloat16)

    lanes = 128
    lane = lax.broadcasted_iota(jnp.int32, (1, lanes), 1)
    lane_u = lane // heads
    sum_row = lax.broadcasted_iota(jnp.int32, (inner, lanes), 0) // HD
    sum_col = lax.broadcasted_iota(jnp.int32, (inner, lanes), 1)
    spread_row = lax.broadcasted_iota(jnp.int32, (lanes, inner), 0)
    spread_col = lax.broadcasted_iota(jnp.int32, (lanes, inner), 1) // HD
    collect = [(sum_row + u * heads == sum_col).astype(jnp.bfloat16) for u in range(var_count)]
    spread = [(spread_col + u * heads == spread_row).astype(jnp.bfloat16) for u in range(var_count)]
    own_id = jnp.full((1, lanes), -2, jnp.int32)
    for u in range(var_count):
        own_id = jnp.where(lane_u == u, ids[u], own_id)
    keys = kbuf[...].reshape(count, rows, inner)
    score = 0.0
    for u in range(var_count):
        product = keys * qbuf[u * rows : (u + 1) * rows, :][None]
        score = score + jnp.dot(
            product.reshape(count * rows, inner), collect[u], preferred_element_type=jnp.float32
        )
    scores = [
        jnp.where(own_id == ids[w], score[w * rows : (w + 1) * rows], -jnp.inf) for w in range(count)
    ]
    highest = functools.reduce(jnp.maximum, scores)
    highest = jnp.where(lane_u < var_count, highest, 0.0)
    raised = [jnp.exp(one - highest) for one in scores]
    total = functools.reduce(lambda a, b: a + b, raised)
    share = 1.0 / jnp.where(lane_u < var_count, total, 1.0)
    prob = jnp.concatenate([(one * share).astype(jnp.bfloat16) for one in raised], axis=0)
    for u in range(var_count):
        each = jnp.dot(prob, spread[u], preferred_element_type=jnp.float32)
        mixed = None
        for w in range(count):
            if needed(u, w, var_count, far_count):
                at = slice(w * rows, (w + 1) * rows)
                term = each[at] * vbuf[at, :].astype(jnp.float32)
                mixed = term if mixed is None else mixed + term
        att[u * rows : (u + 1) * rows, :] = mixed.astype(jnp.bfloat16)
    summed = jnp.dot(att[...], uall[...], preferred_element_type=jnp.float32)
    summed = summed + mid_ref[...].astype(jnp.float32).reshape(summed.shape)
    out_ref[...] = summed.astype(jnp.bfloat16).reshape(out_ref.shape)


def routes(var_size, patch_size):
    def route(even, odd):
        pairs = []
        for v in range(var_size):
            for p in range(patch_size):
                step = odd if v % 2 else even
                pairs.append((v * patch_size + p, v * patch_size + (p ^ step)))
        return pairs
    return route(1, 2), route(2, 1), route(3, 3)


def tied(blocks, after):
    return lax.optimization_barrier((*blocks, after))


def pairs_of(size, partner):
    return [(i, partner(i)) for i in range(size) if 0 <= partner(i) < size]


def on_device(
    tokens, patch_mask, group_ids, time_gain, time_qkv, time_out, space_gain, space_qkv, space_out
):
    var_size, patch_size = lax.axis_size("var"), lax.axis_size("patch")
    var_index, patch_index = lax.axis_index("var"), lax.axis_index("patch")
    core = var_index % 2
    both = ("var", "patch")
    first, second, third = routes(var_size, patch_size)
    swap = pairs_of(var_size, lambda i: i ^ 1)

    def send(block, route):
        return lax.ppermute(block, both, route)

    def partner(block):
        return lax.ppermute(block, "var", swap)

    tok = jnp.transpose(tokens, (1, 0, 2))
    mask = jnp.transpose(patch_mask)
    qkv_t = jnp.transpose(time_qkv, (1, 2, 0))
    qkv_s = jnp.transpose(space_qkv, (1, 2, 0))
    var_count, rows, depth = tok.shape
    kind, width, _ = qkv_t.shape
    half = width // 2

    tok1, tok2 = send(tok, first), send(tok, second)
    mask1, mask2, mask3 = send(mask, first), send(mask, second), send(mask, third)
    tok1f, mask1, mask2, mask3 = lax.optimization_barrier((tok1, mask1, mask2, mask3))
    tok3 = send(tok1f, second)
    weight = qkv_t.reshape(kind * width, depth)
    bf = jnp.bfloat16
    early = pl.pallas_call(
        project_kernel,
        out_shape=jax.ShapeDtypeStruct((3 * var_count * rows, kind * width), bf),
        in_specs=[VM] * 5,
        out_specs=VM,
        compiler_params=params(),
        cost_estimate=cost(1000, 1000),
        name="project",
    )(tok, tok1f, tok2, time_gain, weight)

    far_count = var_count - 1
    level = (var_index // 2) % 2
    place = jnp.stack([core, 1 - level, var_index]).astype(jnp.int32)
    piece = jax.ShapeDtypeStruct((kind + 1, half, depth), bf)
    mine, other = pl.pallas_call(
        split_kernel,
        out_shape=[piece] * 2,
        in_specs=[SM] + [HB] * 2,
        out_specs=[HB] * 2,
        scratch_shapes=[pltpu.SemaphoreType.DMA((4,))],
        compiler_params=params(1),
        cost_estimate=cost(1000, 1000),
        name="split",
    )(place, qkv_s, space_out)
    t_own, mine, other, early = lax.optimization_barrier((time_out[None], mine, other, early))
    t1, c1 = send(t_own, first), send(mine, second)

    near, far_step = jnp.where(core == 0, 1, 2), jnp.where(core == 0, 2, 1)
    bases = jnp.stack(
        [patch_index, patch_index ^ near, patch_index ^ far_step, patch_index ^ 3]
    ).astype(jnp.int32) * rows
    block = jax.ShapeDtypeStruct((var_count, rows, width), bf)
    att = pl.pallas_call(
        time_kernel,
        out_shape=[block, block, jax.ShapeDtypeStruct((2 * var_count, rows, width), bf)],
        in_specs=[SM] + [VM] * 8,
        out_specs=[VM] * 3,
        compiler_params=params(),
        cost_estimate=cost(10_000_000_000, 1000),
        name="time",
    )(bases, early, tok3, mask, mask1, mask2, mask3, time_gain, weight)
    att0, att2, att13 = att
    got = send(att13, first)
    whole = jax.ShapeDtypeStruct((var_count, rows, depth), jnp.bfloat16)
    part = jax.ShapeDtypeStruct((far_count, rows, depth), jnp.bfloat16)
    partial = pl.pallas_call(
        part_kernel,
        out_shape=whole,
        in_specs=[VM] * 4,
        out_specs=VM,
        compiler_params=params(),
        cost_estimate=cost(1000, 1000),
        name="part",
    )(att2, got, time_out, t1)
    partial = send(partial, second)
    other, partial = lax.optimization_barrier((other, partial))
    o1 = send(other, second)
    mid, x_own = pl.pallas_call(
        mid_kernel,
        out_shape=[whole, whole],
        in_specs=[SM] + [VM] * 7,
        out_specs=[VM] * 2,
        compiler_params=params(),
        cost_estimate=cost(1000, 1000),
        name="mid",
    )(place, att0, got, time_out, t1, partial, tok, space_gain)

    got1 = lax.ppermute(x_own, "var", pairs_of(var_size, lambda i: i ^ 2))
    got2 = lax.ppermute(
        x_own, "var", pairs_of(var_size, lambda i: i + 2 if (i // 2) % 2 else i - 2)
    )
    x_swap = partner(x_own)
    c1f, _ = lax.optimization_barrier((c1, x_own))
    c3 = send(c1f, first)
    swapped1, swapped2 = partner(got1), partner(got2)
    c1, o1, got1, got2 = lax.optimization_barrier((c1, o1, got1, got2))
    c2, o2 = partner(c1), partner(o1)
    o3 = partner(c3)
    count = 3 * var_count + 2 * far_count
    own_rows = var_count * rows
    window = pl.pallas_call(
        window_kernel,
        out_shape=jax.ShapeDtypeStruct((count, rows, depth), bf),
        in_specs=[SM] + [VM] * 6,
        out_specs=VM,
        compiler_params=params(8),
        cost_estimate=cost(1000, 1000),
        name="window",
    )(place, x_own, x_swap, got1, got2, swapped1, swapped2)
    inner = 4 * width
    out = pl.pallas_call(
        functools.partial(space_kernel, var_count),
        out_shape=whole,
        in_specs=[SM] * 2 + [VM] * 10,
        out_specs=VM,
        scratch_shapes=[
            pltpu.VMEM((kind, inner, depth), bf),
            pltpu.VMEM((inner, depth), bf),
            pltpu.VMEM((own_rows, inner), bf),
            pltpu.VMEM((count * rows, inner), bf),
            pltpu.VMEM((count * rows, inner), bf),
            pltpu.VMEM((own_rows, inner), bf),
        ],
        compiler_params=params(28),
        cost_estimate=cost(1000, 1000),
        name="space",
    )(place, group_ids, window, qkv_s, space_out, c1, o1, c2, o2, c3, o3, mid)
    return jnp.transpose(out, (1, 0, 2))


def solution(mesh):
    in_specs = (
        P("patch", ("parts", "var"), None),
        P("patch", ("parts", "var")),
        P("parts"),
        P(),
        P(None, None, "patch"),
        P("patch", None),
        P(),
        P(None, None, "patch"),
        P("patch", None),
    )
    out_specs = P("patch", ("parts", "var"), None)
    return jax.shard_map(
        on_device, mesh=mesh, in_specs=in_specs, out_specs=out_specs, check_vma=False
    )
```

```python
import functools

import jax
import jax.numpy as jnp
from jax import lax
from jax.experimental import pallas as pl
from jax.experimental.pallas import tpu as pltpu
from jax.sharding import PartitionSpec as P

HD = 64
SPACE_COST = 10_000_000_000
epsilon = 1e-06
NT = (((1,), (1,)), ((), ()))
VM = pl.BlockSpec(memory_space=pltpu.VMEM)
SM = pl.BlockSpec(memory_space=pltpu.SMEM)
HB = pl.BlockSpec(memory_space=pltpu.HBM)


def params(mib=20):
    return pltpu.CompilerParams(vmem_limit_bytes=mib * 1024 * 1024)


def cost(flops, size):
    return pl.CostEstimate(flops=flops, bytes_accessed=size, transcendentals=0)


def normed(floats, gain):
    mean = jnp.mean(floats * floats, axis=-1, keepdims=True)
    gain = gain.reshape(1, -1)
    return (floats * lax.rsqrt(mean + epsilon) * gain).astype(jnp.bfloat16)


def dot_nt(a, b):
    return lax.dot_general(a, b, NT, preferred_element_type=jnp.float32)


def project_kernel(t0, t1, t2, gain_ref, w_ref, out_ref):
    var_count, rows, depth = t0.shape
    gain = gain_ref[...]
    x = [normed(t[v].astype(jnp.float32), gain) for v in range(var_count) for t in (t0, t1, t2)]
    x = jnp.concatenate(x, axis=0)
    out_ref[...] = dot_nt(x, w_ref[...]).astype(jnp.bfloat16)


def time_kernel(
    base_ref, early_ref, t3, m0, m1, m2, m3, gain_ref, w_ref, o0, o2, o13
):
    masks = (m0, m1, m2, m3)
    var_count, rows, depth = t3.shape
    width = w_ref.shape[0] // 3
    blocks = len(masks)
    total = rows * blocks
    gain = gain_ref[...]
    x = jnp.concatenate([normed(t3[v].astype(jnp.float32), gain) for v in range(var_count)], axis=0)
    late = dot_nt(x, w_ref[...]).astype(jnp.bfloat16)
    row = lax.broadcasted_iota(jnp.int32, (total, total), 0)
    col = lax.broadcasted_iota(jnp.int32, (total, total), 1)

    def positions(index):
        where = index + base_ref[0]
        for block in range(1, blocks):
            shift = base_ref[block] - block * rows
            where = jnp.where(index >= block * rows, index + shift, where)
        return where

    query_pos, key_pos = positions(row), positions(col)
    causal, same = key_pos <= query_pos, key_pos == query_pos
    head_of = lax.broadcasted_iota(jnp.int32, (1, width), 1) // HD
    marks = jnp.concatenate([m[...] for m in masks], axis=1)
    early = rows * (blocks - 1)
    for v in range(var_count):
        projected = jnp.concatenate(
            [early_ref[v * early : (v + 1) * early], late[v * rows : (v + 1) * rows]], axis=0
        )
        queries = projected[:, :width] * jnp.bfloat16(HD ** (-0.5))
        keys = projected[:, width : 2 * width]
        values = projected[:, 2 * width :]
        observed = marks[v : v + 1, :] > 0
        bias = jnp.where(causal & (observed | same), 0.0, -jnp.inf)
        attended = jnp.zeros((total, width), jnp.float32)
        for head in range(width // HD):
            mine = head_of == head
            scores = dot_nt(jnp.where(mine, queries, 0), keys) + bias
            raised = jnp.exp(scores - jnp.max(scores, axis=-1, keepdims=True))
            share = 1.0 / jnp.sum(raised, axis=-1, keepdims=True)
            weights = raised.astype(jnp.bfloat16)
            mixed = jnp.dot(weights, values, preferred_element_type=jnp.float32) * share
            attended = jnp.where(mine, mixed, attended)
        attended = attended.astype(jnp.bfloat16)
        places = (o0.at[v], o13.at[v], o2.at[v], o13.at[var_count + v])
        for block, out in enumerate(places):
            out[...] = attended[block * rows : (block + 1) * rows]


def part_kernel(a2, got, w0, w1, out_ref):
    var_count, rows, width = a2.shape
    own = a2[...].reshape(var_count * rows, width)
    other = got[var_count:].reshape(var_count * rows, width)
    summed = jnp.dot(own, w0[...], preferred_element_type=jnp.float32)
    summed = summed + jnp.dot(other, w1[0], preferred_element_type=jnp.float32)
    out_ref[...] = summed.astype(jnp.bfloat16).reshape(out_ref.shape)


def mid_kernel(
    place_ref, a0, got, w0, w1, part_ref, tok_ref, gain_ref, mid_ref, x_ref
):
    var_count, rows, depth = tok_ref.shape
    width = a0.shape[2]
    gain = gain_ref[...]
    own = a0[...].reshape(var_count * rows, width)
    other = got[:var_count].reshape(var_count * rows, width)
    summed = part_ref[...].astype(jnp.float32).reshape(var_count * rows, depth)
    summed = summed + jnp.dot(own, w0[...], preferred_element_type=jnp.float32)
    summed = summed + jnp.dot(other, w1[0], preferred_element_type=jnp.float32)
    mid = tok_ref[...].astype(jnp.float32).reshape(var_count * rows, depth) + summed
    mid = mid.astype(jnp.bfloat16)
    x_ref[...] = normed(mid.astype(jnp.float32), gain).reshape(tok_ref.shape)
    mid_ref[...] = mid.reshape(tok_ref.shape)


def split_kernel(place_ref, qkv_hbm, u_hbm, mine_hbm, other_hbm, sems):
    kinds, half, core = qkv_hbm.shape[0], mine_hbm.shape[1], place_ref[0]
    copies = []
    for target, index in ((mine_hbm, core), (other_hbm, 1 - core)):
        at = pl.multiple_of(index * half, 32)
        for source, part in (
            (qkv_hbm.at[:, pl.ds(at, half)], target.at[:kinds]),
            (u_hbm.at[pl.ds(at, half)], target.at[kinds]),
        ):
            copies.append(pltpu.make_async_copy(source, part, sems.at[len(copies)]))
            copies[-1].start()
    for copy in copies:
        copy.wait()


def needed(u, w, var_count, far_count):
    if w < 3 * var_count:
        return True
    w -= 3 * var_count
    if w < far_count:
        offset = u + 2 * var_count - (var_count - far_count) - w
    else:
        offset = 2 * var_count + (w - far_count) - u
    return offset <= 2 * var_count - 1


def join_halves(place_ref, first, second, target, at):
    half = first.shape[0]
    core = place_ref[0]
    target[pl.ds(pl.multiple_of(at + core * half, 32), half), :] = first[...]
    target[pl.ds(pl.multiple_of(at + (1 - core) * half, 32), half), :] = second[...]


def window_kernel(place_ref, x0, xs, got1, got2, swapped1, swapped2, xall):
    var_count = x0.shape[0]
    core, up_first = place_ref[0], place_ref[1] == 1
    xall[:var_count] = x0[...]
    xall[var_count : 2 * var_count] = xs[...]
    other_first = up_first == (core == 1)
    xall[2 * var_count : 3 * var_count] = jnp.where(other_first, swapped1[...], swapped2[...])
    at = 3 * var_count
    xall[at : at + var_count - 1] = jnp.where(up_first, got2[1:], got1[1:])
    at += var_count - 1
    xall[at : at + var_count - 1] = jnp.where(up_first, got1[:-1], got2[:-1])


def space_kernel(
    var_count, place_ref, ids_ref, xall, own, u_own, c1, o1, c2, o2, c3, o3, mid_ref,
    out_ref, wall, uall, qbuf, kbuf, vbuf, att,
):
    count, rows, depth = xall.shape
    far_count = var_count - 1
    inner = wall.shape[1]
    core = place_ref[0]
    width = u_own.shape[0]
    for kind in range(4):
        target = wall.at[kind] if kind < 3 else uall
        target[:width, :] = own[kind] if kind < 3 else u_own[...]
        join_halves(place_ref, c1.at[kind], o1.at[kind], target, width)
        join_halves(place_ref, o2.at[kind], c2.at[kind], target, 2 * width)
        join_halves(place_ref, c3.at[kind], o3.at[kind], target, 3 * width)
    heads = inner // HD

    variate = place_ref[2] * var_count
    starts = (0, (1 - 2 * core) * var_count, (2 * core - 1) * var_count)
    offsets = [start + u for start in starts for u in range(var_count)]
    offsets += [u - var_count - far_count for u in range(far_count)]
    offsets += [u + 2 * var_count for u in range(far_count)]
    ids = []
    for offset in offsets:
        at = variate + offset
        inside = (at >= 0) & (at < ids_ref.shape[0])
        ids.append(jnp.where(inside, ids_ref[jnp.clip(at, 0, ids_ref.shape[0] - 1)], -1))

    scaled = dot_nt(xall[:var_count].reshape(var_count * rows, depth), wall[0]).astype(jnp.bfloat16)
    qbuf[...] = scaled * jnp.bfloat16(HD ** (-0.5))
    x_all = xall[...].reshape(count * rows, depth)
    kbuf[...] = dot_nt(x_all, wall[1]).astype(jnp.bfloat16)
    vbuf[...] = dot_nt(x_all, wall[2]).astype(jnp.bfloat16)

    lanes = 128
    lane = lax.broadcasted_iota(jnp.int32, (1, lanes), 1)
    lane_u = lane // heads
    sum_row = lax.broadcasted_iota(jnp.int32, (inner, lanes), 0) // HD
    sum_col = lax.broadcasted_iota(jnp.int32, (inner, lanes), 1)
    spread_row = lax.broadcasted_iota(jnp.int32, (lanes, inner), 0)
    spread_col = lax.broadcasted_iota(jnp.int32, (lanes, inner), 1) // HD
    collect = [(sum_row + u * heads == sum_col).astype(jnp.bfloat16) for u in range(var_count)]
    spread = [(spread_col + u * heads == spread_row).astype(jnp.bfloat16) for u in range(var_count)]
    own_id = jnp.full((1, lanes), -2, jnp.int32)
    for u in range(var_count):
        own_id = jnp.where(lane_u == u, ids[u], own_id)
    reach = [
        [w for w in range(count) if needed(u, w, var_count, far_count)] for u in range(var_count)
    ]
    score = [0.0] * count
    for u in range(var_count):
        query = qbuf[u * rows : (u + 1) * rows, :]
        product = [kbuf[w * rows : (w + 1) * rows, :] * query for w in reach[u]]
        part = jnp.dot(
            jnp.concatenate(product, axis=0), collect[u], preferred_element_type=jnp.float32
        )
        for place, w in enumerate(reach[u]):
            score[w] = score[w] + part[place * rows : (place + 1) * rows]
    scores = [
        jnp.where(own_id == ids[w], score[w], -jnp.inf) for w in range(count)
    ]
    highest = functools.reduce(jnp.maximum, scores)
    highest = jnp.where(lane_u < var_count, highest, 0.0)
    raised = [jnp.exp(one - highest) for one in scores]
    total = functools.reduce(lambda a, b: a + b, raised)
    share = 1.0 / jnp.where(lane_u < var_count, total, 1.0)
    prob = [(one * share).astype(jnp.bfloat16) for one in raised]
    for u in range(var_count):
        shares = jnp.concatenate([prob[w] for w in reach[u]], axis=0)
        each = jnp.dot(shares, spread[u], preferred_element_type=jnp.float32)
        mixed = None
        for place, w in enumerate(reach[u]):
            values = vbuf[w * rows : (w + 1) * rows, :].astype(jnp.float32)
            term = each[place * rows : (place + 1) * rows] * values
            mixed = term if mixed is None else mixed + term
        att[u * rows : (u + 1) * rows, :] = mixed.astype(jnp.bfloat16)
    summed = jnp.dot(att[...], uall[...], preferred_element_type=jnp.float32)
    summed = summed + mid_ref[...].astype(jnp.float32).reshape(summed.shape)
    out_ref[...] = summed.astype(jnp.bfloat16).reshape(out_ref.shape)


def routes(var_size, patch_size):
    def route(even, odd):
        pairs = []
        for v in range(var_size):
            for p in range(patch_size):
                step = odd if v % 2 else even
                pairs.append((v * patch_size + p, v * patch_size + (p ^ step)))
        return pairs
    return route(1, 2), route(2, 1), route(3, 3)


def tied(blocks, after):
    return lax.optimization_barrier((*blocks, after))


def pairs_of(size, partner):
    return [(i, partner(i)) for i in range(size) if 0 <= partner(i) < size]


def on_device(
    tokens, patch_mask, group_ids, time_gain, time_qkv, time_out, space_gain, space_qkv, space_out
):
    var_size, patch_size = lax.axis_size("var"), lax.axis_size("patch")
    var_index, patch_index = lax.axis_index("var"), lax.axis_index("patch")
    core = var_index % 2
    both = ("var", "patch")
    first, second, third = routes(var_size, patch_size)
    swap = pairs_of(var_size, lambda i: i ^ 1)

    def send(block, route):
        return lax.ppermute(block, both, route)

    def partner(block):
        return lax.ppermute(block, "var", swap)

    tok = jnp.transpose(tokens, (1, 0, 2))
    mask = jnp.transpose(patch_mask)
    qkv_t = jnp.transpose(time_qkv, (1, 2, 0))
    qkv_s = jnp.transpose(space_qkv, (1, 2, 0))
    var_count, rows, depth = tok.shape
    kind, width, _ = qkv_t.shape
    half = width // 2

    tok1, tok2 = send(tok, first), send(tok, second)
    mask1, mask2, mask3 = send(mask, first), send(mask, second), send(mask, third)
    tok1f, mask1, mask2, mask3 = lax.optimization_barrier((tok1, mask1, mask2, mask3))
    tok3 = send(tok1f, second)
    weight = qkv_t.reshape(kind * width, depth)
    bf = jnp.bfloat16
    early = pl.pallas_call(
        project_kernel,
        out_shape=jax.ShapeDtypeStruct((3 * var_count * rows, kind * width), bf),
        in_specs=[VM] * 5,
        out_specs=VM,
        compiler_params=params(),
        cost_estimate=cost(1000, 1000),
        name="project",
    )(tok, tok1f, tok2, time_gain, weight)

    far_count = var_count - 1
    level = (var_index // 2) % 2
    place = jnp.stack([core, 1 - level, var_index]).astype(jnp.int32)
    piece = jax.ShapeDtypeStruct((kind + 1, half, depth), bf)
    mine, other = pl.pallas_call(
        split_kernel,
        out_shape=[piece] * 2,
        in_specs=[SM] + [HB] * 2,
        out_specs=[HB] * 2,
        scratch_shapes=[pltpu.SemaphoreType.DMA((4,))],
        compiler_params=params(1),
        cost_estimate=cost(1000, 1000),
        name="split",
    )(place, qkv_s, space_out)
    t_own, mine, other, early = lax.optimization_barrier((time_out[None], mine, other, early))
    t1, c1 = send(t_own, first), send(mine, second)

    near, far_step = jnp.where(core == 0, 1, 2), jnp.where(core == 0, 2, 1)
    bases = jnp.stack(
        [patch_index, patch_index ^ near, patch_index ^ far_step, patch_index ^ 3]
    ).astype(jnp.int32) * rows
    block = jax.ShapeDtypeStruct((var_count, rows, width), bf)
    att = pl.pallas_call(
        time_kernel,
        out_shape=[block, block, jax.ShapeDtypeStruct((2 * var_count, rows, width), bf)],
        in_specs=[SM] + [VM] * 8,
        out_specs=[VM] * 3,
        compiler_params=params(),
        cost_estimate=cost(10_000_000_000, 1000),
        name="time",
    )(bases, early, tok3, mask, mask1, mask2, mask3, time_gain, weight)
    att0, att2, att13 = att
    got = send(att13, first)
    whole = jax.ShapeDtypeStruct((var_count, rows, depth), jnp.bfloat16)
    part = jax.ShapeDtypeStruct((far_count, rows, depth), jnp.bfloat16)
    partial = pl.pallas_call(
        part_kernel,
        out_shape=whole,
        in_specs=[VM] * 4,
        out_specs=VM,
        compiler_params=params(),
        cost_estimate=cost(1000, 1000),
        name="part",
    )(att2, got, time_out, t1)
    partial = send(partial, second)
    other, partial = lax.optimization_barrier((other, partial))
    o1 = send(other, second)
    mid, x_own = pl.pallas_call(
        mid_kernel,
        out_shape=[whole, whole],
        in_specs=[SM] + [VM] * 7,
        out_specs=[VM] * 2,
        compiler_params=params(),
        cost_estimate=cost(1000, 1000),
        name="mid",
    )(place, att0, got, time_out, t1, partial, tok, space_gain)

    got1 = lax.ppermute(x_own, "var", pairs_of(var_size, lambda i: i ^ 2))
    got2 = lax.ppermute(
        x_own, "var", pairs_of(var_size, lambda i: i + 2 if (i // 2) % 2 else i - 2)
    )
    x_swap = partner(x_own)
    c1f, _ = lax.optimization_barrier((c1, x_own))
    c3 = send(c1f, first)
    swapped1, swapped2 = partner(got1), partner(got2)
    c2 = partner(c1f)
    o1, got1, got2 = lax.optimization_barrier((o1, got1, got2))
    o2 = partner(o1)
    o3 = partner(c3)
    count = 3 * var_count + 2 * far_count
    own_rows = var_count * rows
    window = pl.pallas_call(
        window_kernel,
        out_shape=jax.ShapeDtypeStruct((count, rows, depth), bf),
        in_specs=[SM] + [VM] * 6,
        out_specs=VM,
        compiler_params=params(8),
        cost_estimate=cost(1000, 1000),
        name="window",
    )(place, x_own, x_swap, got1, got2, swapped1, swapped2)
    inner = 4 * width
    out = pl.pallas_call(
        functools.partial(space_kernel, var_count),
        out_shape=whole,
        in_specs=[SM] * 2 + [VM] * 10,
        out_specs=VM,
        scratch_shapes=[
            pltpu.VMEM((kind, inner, depth), bf),
            pltpu.VMEM((inner, depth), bf),
            pltpu.VMEM((own_rows, inner), bf),
            pltpu.VMEM((count * rows, inner), bf),
            pltpu.VMEM((count * rows, inner), bf),
            pltpu.VMEM((own_rows, inner), bf),
        ],
        compiler_params=params(28),
        cost_estimate=cost(1000, 1000),
        name="space",
    )(place, group_ids, window, qkv_s, space_out, c1, o1, c2, o2, c3, o3, mid)
    return jnp.transpose(out, (1, 0, 2))


def solution(mesh):
    in_specs = (
        P("patch", ("parts", "var"), None),
        P("patch", ("parts", "var")),
        P("parts"),
        P(),
        P(None, None, "patch"),
        P("patch", None),
        P(),
        P(None, None, "patch"),
        P("patch", None),
    )
    out_specs = P("patch", ("parts", "var"), None)
    return jax.shard_map(
        on_device, mesh=mesh, in_specs=in_specs, out_specs=out_specs, check_vma=False
    )
```

```python
import functools

import jax
import jax.numpy as jnp
from jax import lax
from jax.experimental import pallas as pl
from jax.experimental.pallas import tpu as pltpu
from jax.sharding import PartitionSpec as P

HD = 64
SPACE_COST = 10_000_000_000
epsilon = 1e-06
NT = (((1,), (1,)), ((), ()))
VM = pl.BlockSpec(memory_space=pltpu.VMEM)
SM = pl.BlockSpec(memory_space=pltpu.SMEM)
HB = pl.BlockSpec(memory_space=pltpu.HBM)


def params(mib=20):
    return pltpu.CompilerParams(vmem_limit_bytes=mib * 1024 * 1024)


def cost(flops, size):
    return pl.CostEstimate(flops=flops, bytes_accessed=size, transcendentals=0)


def normed(floats, gain):
    mean = jnp.mean(floats * floats, axis=-1, keepdims=True)
    gain = gain.reshape(1, -1)
    return (floats * lax.rsqrt(mean + epsilon) * gain).astype(jnp.bfloat16)


def dot_nt(a, b):
    return lax.dot_general(a, b, NT, preferred_element_type=jnp.float32)


def project_kernel(t0, t1, t2, gain_ref, w_ref, out_ref):
    var_count, rows, depth = t0.shape
    gain = gain_ref[...]
    x = [normed(t[v].astype(jnp.float32), gain) for v in range(var_count) for t in (t0, t1, t2)]
    x = jnp.concatenate(x, axis=0)
    out_ref[...] = dot_nt(x, w_ref[...]).astype(jnp.bfloat16)


def time_kernel(
    base_ref, early_ref, t3, m0, m1, m2, m3, gain_ref, w_ref, o0, o2, o13
):
    masks = (m0, m1, m2, m3)
    var_count, rows, depth = t3.shape
    width = w_ref.shape[0] // 3
    blocks = len(masks)
    total = rows * blocks
    gain = gain_ref[...]
    x = jnp.concatenate([normed(t3[v].astype(jnp.float32), gain) for v in range(var_count)], axis=0)
    late = dot_nt(x, w_ref[...]).astype(jnp.bfloat16)
    row = lax.broadcasted_iota(jnp.int32, (total, total), 0)
    col = lax.broadcasted_iota(jnp.int32, (total, total), 1)

    def positions(index):
        where = index + base_ref[0]
        for block in range(1, blocks):
            shift = base_ref[block] - block * rows
            where = jnp.where(index >= block * rows, index + shift, where)
        return where

    query_pos, key_pos = positions(row), positions(col)
    causal, same = key_pos <= query_pos, key_pos == query_pos
    head_of = lax.broadcasted_iota(jnp.int32, (1, width), 1) // HD
    marks = jnp.concatenate([m[...] for m in masks], axis=1)
    early = rows * (blocks - 1)
    for v in range(var_count):
        projected = jnp.concatenate(
            [early_ref[v * early : (v + 1) * early], late[v * rows : (v + 1) * rows]], axis=0
        )
        queries = projected[:, :width] * jnp.bfloat16(HD ** (-0.5))
        keys = projected[:, width : 2 * width]
        values = projected[:, 2 * width :]
        observed = marks[v : v + 1, :] > 0
        bias = jnp.where(causal & (observed | same), 0.0, -jnp.inf)
        attended = jnp.zeros((total, width), jnp.float32)
        for head in range(width // HD):
            mine = head_of == head
            scores = dot_nt(jnp.where(mine, queries, 0), keys) + bias
            raised = jnp.exp(scores - jnp.max(scores, axis=-1, keepdims=True))
            share = 1.0 / jnp.sum(raised, axis=-1, keepdims=True)
            weights = raised.astype(jnp.bfloat16)
            mixed = jnp.dot(weights, values, preferred_element_type=jnp.float32) * share
            attended = jnp.where(mine, mixed, attended)
        attended = attended.astype(jnp.bfloat16)
        places = (o0.at[v], o13.at[v], o2.at[v], o13.at[var_count + v])
        for block, out in enumerate(places):
            out[...] = attended[block * rows : (block + 1) * rows]


def part_kernel(a2, got, w0, w1, out_ref):
    var_count, rows, width = a2.shape
    own = a2[...].reshape(var_count * rows, width)
    other = got[var_count:].reshape(var_count * rows, width)
    summed = jnp.dot(own, w0[...], preferred_element_type=jnp.float32)
    summed = summed + jnp.dot(other, w1[0], preferred_element_type=jnp.float32)
    out_ref[...] = summed.astype(jnp.bfloat16).reshape(out_ref.shape)


def mid_kernel(
    place_ref, a0, got, w0, w1, part_ref, tok_ref, gain_ref, mid_ref, x_ref
):
    var_count, rows, depth = tok_ref.shape
    width = a0.shape[2]
    gain = gain_ref[...]
    own = a0[...].reshape(var_count * rows, width)
    other = got[:var_count].reshape(var_count * rows, width)
    summed = part_ref[...].astype(jnp.float32).reshape(var_count * rows, depth)
    summed = summed + jnp.dot(own, w0[...], preferred_element_type=jnp.float32)
    summed = summed + jnp.dot(other, w1[0], preferred_element_type=jnp.float32)
    mid = tok_ref[...].astype(jnp.float32).reshape(var_count * rows, depth) + summed
    mid = mid.astype(jnp.bfloat16)
    x_ref[...] = normed(mid.astype(jnp.float32), gain).reshape(tok_ref.shape)
    mid_ref[...] = mid.reshape(tok_ref.shape)


def split_kernel(place_ref, qkv_hbm, u_hbm, mine_hbm, other_hbm, sems):
    kinds, half, core = qkv_hbm.shape[0], mine_hbm.shape[1], place_ref[0]
    copies = []
    for target, index in ((mine_hbm, core), (other_hbm, 1 - core)):
        at = pl.multiple_of(index * half, 32)
        for source, part in (
            (qkv_hbm.at[:, pl.ds(at, half)], target.at[:kinds]),
            (u_hbm.at[pl.ds(at, half)], target.at[kinds]),
        ):
            copies.append(pltpu.make_async_copy(source, part, sems.at[len(copies)]))
            copies[-1].start()
    for copy in copies:
        copy.wait()


def needed(u, w, var_count, far_count):
    if w < 3 * var_count:
        return True
    w -= 3 * var_count
    if w < far_count:
        offset = u + 2 * var_count - (var_count - far_count) - w
    else:
        offset = 2 * var_count + (w - far_count) - u
    return offset <= 2 * var_count - 1


def join_halves(place_ref, first, second, target, at):
    half = first.shape[0]
    core = place_ref[0]
    target[pl.ds(pl.multiple_of(at + core * half, 32), half), :] = first[...]
    target[pl.ds(pl.multiple_of(at + (1 - core) * half, 32), half), :] = second[...]


def gather_window(place_ref, x0, xs, got1, got2, swapped1, swapped2, xall):
    var_count = x0.shape[0]
    core, up_first = place_ref[0], place_ref[1] == 1
    xall[:var_count] = x0[...]
    xall[var_count : 2 * var_count] = xs[...]
    other_first = up_first == (core == 1)
    xall[2 * var_count : 3 * var_count] = jnp.where(other_first, swapped1[...], swapped2[...])
    at = 3 * var_count
    xall[at : at + var_count - 1] = jnp.where(up_first, got2[1:], got1[1:])
    at += var_count - 1
    xall[at : at + var_count - 1] = jnp.where(up_first, got1[:-1], got2[:-1])


def space_kernel(
    var_count, place_ref, ids_ref, x0, xs, got1, got2, swapped1, swapped2,
    own, u_own, c1, o1, c2, o2, c3, o3, mid_ref,
    out_ref, xall, wall, uall, qbuf, kbuf, vbuf, att,
):
    count, rows, depth = xall.shape
    far_count = var_count - 1
    inner = wall.shape[1]
    core = place_ref[0]
    width = u_own.shape[0]
    gather_window(place_ref, x0, xs, got1, got2, swapped1, swapped2, xall)
    for kind in range(4):
        target = wall.at[kind] if kind < 3 else uall
        target[:width, :] = own[kind] if kind < 3 else u_own[...]
        join_halves(place_ref, c1.at[kind], o1.at[kind], target, width)
        join_halves(place_ref, o2.at[kind], c2.at[kind], target, 2 * width)
        join_halves(place_ref, c3.at[kind], o3.at[kind], target, 3 * width)
    heads = inner // HD

    variate = place_ref[2] * var_count
    starts = (0, (1 - 2 * core) * var_count, (2 * core - 1) * var_count)
    offsets = [start + u for start in starts for u in range(var_count)]
    offsets += [u - var_count - far_count for u in range(far_count)]
    offsets += [u + 2 * var_count for u in range(far_count)]
    ids = []
    for offset in offsets:
        at = variate + offset
        inside = (at >= 0) & (at < ids_ref.shape[0])
        ids.append(jnp.where(inside, ids_ref[jnp.clip(at, 0, ids_ref.shape[0] - 1)], -1))

    scaled = dot_nt(xall[:var_count].reshape(var_count * rows, depth), wall[0]).astype(jnp.bfloat16)
    qbuf[...] = scaled * jnp.bfloat16(HD ** (-0.5))
    x_all = xall[...].reshape(count * rows, depth)
    kbuf[...] = dot_nt(x_all, wall[1]).astype(jnp.bfloat16)
    vbuf[...] = dot_nt(x_all, wall[2]).astype(jnp.bfloat16)

    lanes = 128
    lane = lax.broadcasted_iota(jnp.int32, (1, lanes), 1)
    lane_u = lane // heads
    sum_row = lax.broadcasted_iota(jnp.int32, (inner, lanes), 0) // HD
    sum_col = lax.broadcasted_iota(jnp.int32, (inner, lanes), 1)
    spread_row = lax.broadcasted_iota(jnp.int32, (lanes, inner), 0)
    spread_col = lax.broadcasted_iota(jnp.int32, (lanes, inner), 1) // HD
    collect = [(sum_row + u * heads == sum_col).astype(jnp.bfloat16) for u in range(var_count)]
    spread = [(spread_col + u * heads == spread_row).astype(jnp.bfloat16) for u in range(var_count)]
    own_id = jnp.full((1, lanes), -2, jnp.int32)
    for u in range(var_count):
        own_id = jnp.where(lane_u == u, ids[u], own_id)
    reach = [
        [w for w in range(count) if needed(u, w, var_count, far_count)] for u in range(var_count)
    ]
    score = [0.0] * count
    for u in range(var_count):
        query = qbuf[u * rows : (u + 1) * rows, :]
        product = [kbuf[w * rows : (w + 1) * rows, :] * query for w in reach[u]]
        part = jnp.dot(
            jnp.concatenate(product, axis=0), collect[u], preferred_element_type=jnp.float32
        )
        for place, w in enumerate(reach[u]):
            score[w] = score[w] + part[place * rows : (place + 1) * rows]
    scores = [
        jnp.where(own_id == ids[w], score[w], -jnp.inf) for w in range(count)
    ]
    highest = functools.reduce(jnp.maximum, scores)
    highest = jnp.where(lane_u < var_count, highest, 0.0)
    raised = [jnp.exp(one - highest) for one in scores]
    total = functools.reduce(lambda a, b: a + b, raised)
    share = 1.0 / jnp.where(lane_u < var_count, total, 1.0)
    prob = [(one * share).astype(jnp.bfloat16) for one in raised]
    for u in range(var_count):
        shares = jnp.concatenate([prob[w] for w in reach[u]], axis=0)
        each = jnp.dot(shares, spread[u], preferred_element_type=jnp.float32)
        mixed = None
        for place, w in enumerate(reach[u]):
            values = vbuf[w * rows : (w + 1) * rows, :].astype(jnp.float32)
            term = each[place * rows : (place + 1) * rows] * values
            mixed = term if mixed is None else mixed + term
        att[u * rows : (u + 1) * rows, :] = mixed.astype(jnp.bfloat16)
    summed = jnp.dot(att[...], uall[...], preferred_element_type=jnp.float32)
    summed = summed + mid_ref[...].astype(jnp.float32).reshape(summed.shape)
    out_ref[...] = summed.astype(jnp.bfloat16).reshape(out_ref.shape)


def routes(var_size, patch_size):
    def route(even, odd):
        pairs = []
        for v in range(var_size):
            for p in range(patch_size):
                step = odd if v % 2 else even
                pairs.append((v * patch_size + p, v * patch_size + (p ^ step)))
        return pairs
    return route(1, 2), route(2, 1), route(3, 3)


def tied(blocks, after):
    return lax.optimization_barrier((*blocks, after))


def pairs_of(size, partner):
    return [(i, partner(i)) for i in range(size) if 0 <= partner(i) < size]


def on_device(
    tokens, patch_mask, group_ids, time_gain, time_qkv, time_out, space_gain, space_qkv, space_out
):
    var_size, patch_size = lax.axis_size("var"), lax.axis_size("patch")
    var_index, patch_index = lax.axis_index("var"), lax.axis_index("patch")
    core = var_index % 2
    both = ("var", "patch")
    first, second, third = routes(var_size, patch_size)
    swap = pairs_of(var_size, lambda i: i ^ 1)

    def send(block, route):
        return lax.ppermute(block, both, route)

    def partner(block):
        return lax.ppermute(block, "var", swap)

    tok = jnp.transpose(tokens, (1, 0, 2))
    mask = jnp.transpose(patch_mask)
    qkv_t = jnp.transpose(time_qkv, (1, 2, 0))
    qkv_s = jnp.transpose(space_qkv, (1, 2, 0))
    var_count, rows, depth = tok.shape
    kind, width, _ = qkv_t.shape
    half = width // 2

    tok1, tok2 = send(tok, first), send(tok, second)
    mask1, mask2, mask3 = send(mask, first), send(mask, second), send(mask, third)
    tok1f, mask1, mask2, mask3 = lax.optimization_barrier((tok1, mask1, mask2, mask3))
    tok3 = send(tok1f, second)
    weight = qkv_t.reshape(kind * width, depth)
    bf = jnp.bfloat16
    early = pl.pallas_call(
        project_kernel,
        out_shape=jax.ShapeDtypeStruct((3 * var_count * rows, kind * width), bf),
        in_specs=[VM] * 5,
        out_specs=VM,
        compiler_params=params(),
        cost_estimate=cost(1000, 1000),
        name="project",
    )(tok, tok1f, tok2, time_gain, weight)

    far_count = var_count - 1
    level = (var_index // 2) % 2
    place = jnp.stack([core, 1 - level, var_index]).astype(jnp.int32)
    piece = jax.ShapeDtypeStruct((kind + 1, half, depth), bf)
    mine, other = pl.pallas_call(
        split_kernel,
        out_shape=[piece] * 2,
        in_specs=[SM] + [HB] * 2,
        out_specs=[HB] * 2,
        scratch_shapes=[pltpu.SemaphoreType.DMA((4,))],
        compiler_params=params(1),
        cost_estimate=cost(1000, 1000),
        name="split",
    )(place, qkv_s, space_out)
    t_own, mine, other, early = lax.optimization_barrier((time_out[None], mine, other, early))
    t1, c1 = send(t_own, first), send(mine, second)

    near, far_step = jnp.where(core == 0, 1, 2), jnp.where(core == 0, 2, 1)
    bases = jnp.stack(
        [patch_index, patch_index ^ near, patch_index ^ far_step, patch_index ^ 3]
    ).astype(jnp.int32) * rows
    block = jax.ShapeDtypeStruct((var_count, rows, width), bf)
    att = pl.pallas_call(
        time_kernel,
        out_shape=[block, block, jax.ShapeDtypeStruct((2 * var_count, rows, width), bf)],
        in_specs=[SM] + [VM] * 8,
        out_specs=[VM] * 3,
        compiler_params=params(),
        cost_estimate=cost(10_000_000_000, 1000),
        name="time",
    )(bases, early, tok3, mask, mask1, mask2, mask3, time_gain, weight)
    att0, att2, att13 = att
    got = send(att13, first)
    whole = jax.ShapeDtypeStruct((var_count, rows, depth), jnp.bfloat16)
    part = jax.ShapeDtypeStruct((far_count, rows, depth), jnp.bfloat16)
    partial = pl.pallas_call(
        part_kernel,
        out_shape=whole,
        in_specs=[VM] * 4,
        out_specs=VM,
        compiler_params=params(),
        cost_estimate=cost(1000, 1000),
        name="part",
    )(att2, got, time_out, t1)
    partial = send(partial, second)
    other, partial = lax.optimization_barrier((other, partial))
    o1 = send(other, second)
    mid, x_own = pl.pallas_call(
        mid_kernel,
        out_shape=[whole, whole],
        in_specs=[SM] + [VM] * 7,
        out_specs=[VM] * 2,
        compiler_params=params(),
        cost_estimate=cost(1000, 1000),
        name="mid",
    )(place, att0, got, time_out, t1, partial, tok, space_gain)

    got1 = lax.ppermute(x_own, "var", pairs_of(var_size, lambda i: i ^ 2))
    got2 = lax.ppermute(
        x_own, "var", pairs_of(var_size, lambda i: i + 2 if (i // 2) % 2 else i - 2)
    )
    x_swap = partner(x_own)
    c1f, _ = lax.optimization_barrier((c1, x_own))
    c3 = send(c1f, first)
    swapped1, swapped2 = partner(got1), partner(got2)
    c2 = partner(c1f)
    o1, got1, got2 = lax.optimization_barrier((o1, got1, got2))
    o2 = partner(o1)
    o3 = partner(c3)
    count = 3 * var_count + 2 * far_count
    own_rows = var_count * rows
    inner = 4 * width
    out = pl.pallas_call(
        functools.partial(space_kernel, var_count),
        out_shape=whole,
        in_specs=[SM] * 2 + [VM] * 15,
        out_specs=VM,
        scratch_shapes=[
            pltpu.VMEM((count, rows, depth), bf),
            pltpu.VMEM((kind, inner, depth), bf),
            pltpu.VMEM((inner, depth), bf),
            pltpu.VMEM((own_rows, inner), bf),
            pltpu.VMEM((count * rows, inner), bf),
            pltpu.VMEM((count * rows, inner), bf),
            pltpu.VMEM((own_rows, inner), bf),
        ],
        compiler_params=params(28),
        cost_estimate=cost(1000, 1000),
        name="space",
    )(place, group_ids, x_own, x_swap, got1, got2, swapped1, swapped2, qkv_s, space_out, c1, o1, c2, o2, c3, o3, mid)
    return jnp.transpose(out, (1, 0, 2))


def solution(mesh):
    in_specs = (
        P("patch", ("parts", "var"), None),
        P("patch", ("parts", "var")),
        P("parts"),
        P(),
        P(None, None, "patch"),
        P("patch", None),
        P(),
        P(None, None, "patch"),
        P("patch", None),
    )
    out_specs = P("patch", ("parts", "var"), None)
    return jax.shard_map(
        on_device, mesh=mesh, in_specs=in_specs, out_specs=out_specs, check_vma=False
    )
```

```python
import functools

import jax
import jax.numpy as jnp
from jax import lax
from jax.experimental import pallas as pl
from jax.experimental.pallas import tpu as pltpu
from jax.sharding import PartitionSpec as P

HD = 64
SPACE_COST = 10_000_000_000
epsilon = 1e-06
NT = (((1,), (1,)), ((), ()))
VM = pl.BlockSpec(memory_space=pltpu.VMEM)
SM = pl.BlockSpec(memory_space=pltpu.SMEM)
HB = pl.BlockSpec(memory_space=pltpu.HBM)


def params(mib=20):
    return pltpu.CompilerParams(vmem_limit_bytes=mib * 1024 * 1024)


def cost(flops, size):
    return pl.CostEstimate(flops=flops, bytes_accessed=size, transcendentals=0)


def normed(floats, gain):
    mean = jnp.mean(floats * floats, axis=-1, keepdims=True)
    gain = gain.reshape(1, -1)
    return (floats * lax.rsqrt(mean + epsilon) * gain).astype(jnp.bfloat16)


def dot_nt(a, b):
    return lax.dot_general(a, b, NT, preferred_element_type=jnp.float32)


def project_kernel(t0, t1, t2, gain_ref, w_ref, m0, m1, m2, m3, out_ref, marks_ref):
    marks_ref[...] = jnp.concatenate([m[...] for m in (m0, m1, m2, m3)], axis=1)
    var_count, rows, depth = t0.shape
    gain = gain_ref[...]
    x = [normed(t[v].astype(jnp.float32), gain) for v in range(var_count) for t in (t0, t1, t2)]
    x = jnp.concatenate(x, axis=0)
    out_ref[...] = dot_nt(x, w_ref[...]).astype(jnp.bfloat16)


def time_kernel(
    base_ref, early_ref, t3, marks_ref, gain_ref, w_ref, o0, o2, o13
):
    var_count, rows, depth = t3.shape
    width = w_ref.shape[0] // 3
    blocks = marks_ref.shape[1] // rows
    total = rows * blocks
    gain = gain_ref[...]
    x = jnp.concatenate([normed(t3[v].astype(jnp.float32), gain) for v in range(var_count)], axis=0)
    late = dot_nt(x, w_ref[...]).astype(jnp.bfloat16)
    row = lax.broadcasted_iota(jnp.int32, (total, total), 0)
    col = lax.broadcasted_iota(jnp.int32, (total, total), 1)

    def positions(index):
        where = index + base_ref[0]
        for block in range(1, blocks):
            shift = base_ref[block] - block * rows
            where = jnp.where(index >= block * rows, index + shift, where)
        return where

    query_pos, key_pos = positions(row), positions(col)
    causal, same = key_pos <= query_pos, key_pos == query_pos
    head_of = lax.broadcasted_iota(jnp.int32, (1, width), 1) // HD
    marks = marks_ref[...]
    early = rows * (blocks - 1)
    for v in range(var_count):
        projected = jnp.concatenate(
            [early_ref[v * early : (v + 1) * early], late[v * rows : (v + 1) * rows]], axis=0
        )
        queries = projected[:, :width] * jnp.bfloat16(HD ** (-0.5))
        keys = projected[:, width : 2 * width]
        values = projected[:, 2 * width :]
        observed = marks[v : v + 1, :] > 0
        bias = jnp.where(causal & (observed | same), 0.0, -jnp.inf)
        attended = jnp.zeros((total, width), jnp.float32)
        for head in range(width // HD):
            mine = head_of == head
            scores = dot_nt(jnp.where(mine, queries, 0), keys) + bias
            raised = jnp.exp(scores - jnp.max(scores, axis=-1, keepdims=True))
            share = 1.0 / jnp.sum(raised, axis=-1, keepdims=True)
            weights = raised.astype(jnp.bfloat16)
            mixed = jnp.dot(weights, values, preferred_element_type=jnp.float32) * share
            attended = jnp.where(mine, mixed, attended)
        attended = attended.astype(jnp.bfloat16)
        places = (o0.at[v], o13.at[v], o2.at[v], o13.at[var_count + v])
        for block, out in enumerate(places):
            out[...] = attended[block * rows : (block + 1) * rows]


def part_kernel(a2, got, w0, w1, out_ref):
    var_count, rows, width = a2.shape
    own = a2[...].reshape(var_count * rows, width)
    other = got[var_count:].reshape(var_count * rows, width)
    summed = jnp.dot(own, w0[...], preferred_element_type=jnp.float32)
    summed = summed + jnp.dot(other, w1[0], preferred_element_type=jnp.float32)
    out_ref[...] = summed.astype(jnp.bfloat16).reshape(out_ref.shape)


def mid_kernel(
    place_ref, a0, got, w0, w1, part_ref, tok_ref, gain_ref, mid_ref, x_ref
):
    var_count, rows, depth = tok_ref.shape
    width = a0.shape[2]
    gain = gain_ref[...]
    own = a0[...].reshape(var_count * rows, width)
    other = got[:var_count].reshape(var_count * rows, width)
    summed = part_ref[...].astype(jnp.float32).reshape(var_count * rows, depth)
    summed = summed + jnp.dot(own, w0[...], preferred_element_type=jnp.float32)
    summed = summed + jnp.dot(other, w1[0], preferred_element_type=jnp.float32)
    mid = tok_ref[...].astype(jnp.float32).reshape(var_count * rows, depth) + summed
    mid = mid.astype(jnp.bfloat16)
    x_ref[...] = normed(mid.astype(jnp.float32), gain).reshape(tok_ref.shape)
    mid_ref[...] = mid.reshape(tok_ref.shape)


def split_kernel(place_ref, qkv_hbm, u_hbm, mine_hbm, other_hbm, sems):
    kinds, half, core = qkv_hbm.shape[0], mine_hbm.shape[1], place_ref[0]
    copies = []
    for target, index in ((mine_hbm, core), (other_hbm, 1 - core)):
        at = pl.multiple_of(index * half, 32)
        for source, part in (
            (qkv_hbm.at[:, pl.ds(at, half)], target.at[:kinds]),
            (u_hbm.at[pl.ds(at, half)], target.at[kinds]),
        ):
            copies.append(pltpu.make_async_copy(source, part, sems.at[len(copies)]))
            copies[-1].start()
    for copy in copies:
        copy.wait()


def needed(u, w, var_count, far_count):
    if w < 3 * var_count:
        return True
    w -= 3 * var_count
    if w < far_count:
        offset = u + 2 * var_count - (var_count - far_count) - w
    else:
        offset = 2 * var_count + (w - far_count) - u
    return offset <= 2 * var_count - 1


def join_halves(place_ref, first, second, target, at):
    half = first.shape[0]
    core = place_ref[0]
    target[pl.ds(pl.multiple_of(at + core * half, 32), half), :] = first[...]
    target[pl.ds(pl.multiple_of(at + (1 - core) * half, 32), half), :] = second[...]


def gather_window(place_ref, x0, xs, got1, got2, swapped1, swapped2, xall):
    var_count = x0.shape[0]
    core, up_first = place_ref[0], place_ref[1] == 1
    xall[:var_count] = x0[...]
    xall[var_count : 2 * var_count] = xs[...]
    other_first = up_first == (core == 1)
    xall[2 * var_count : 3 * var_count] = jnp.where(other_first, swapped1[...], swapped2[...])
    at = 3 * var_count
    xall[at : at + var_count - 1] = jnp.where(up_first, got2[1:], got1[1:])
    at += var_count - 1
    xall[at : at + var_count - 1] = jnp.where(up_first, got1[:-1], got2[:-1])


def space_kernel(
    var_count, place_ref, ids_ref, x0, xs, got1, got2, swapped1, swapped2,
    own, u_own, c1, o1, c2, o2, c3, o3, mid_ref,
    out_ref, xall, wall, uall, qbuf, kbuf, vbuf, att,
):
    count, rows, depth = xall.shape
    far_count = var_count - 1
    inner = wall.shape[1]
    core = place_ref[0]
    width = u_own.shape[0]
    gather_window(place_ref, x0, xs, got1, got2, swapped1, swapped2, xall)
    for kind in range(4):
        target = wall.at[kind] if kind < 3 else uall
        target[:width, :] = own[kind] if kind < 3 else u_own[...]
        join_halves(place_ref, c1.at[kind], o1.at[kind], target, width)
        join_halves(place_ref, o2.at[kind], c2.at[kind], target, 2 * width)
        join_halves(place_ref, c3.at[kind], o3.at[kind], target, 3 * width)
    heads = inner // HD

    variate = place_ref[2] * var_count
    starts = (0, (1 - 2 * core) * var_count, (2 * core - 1) * var_count)
    offsets = [start + u for start in starts for u in range(var_count)]
    offsets += [u - var_count - far_count for u in range(far_count)]
    offsets += [u + 2 * var_count for u in range(far_count)]
    ids = []
    for offset in offsets:
        at = variate + offset
        inside = (at >= 0) & (at < ids_ref.shape[0])
        ids.append(jnp.where(inside, ids_ref[jnp.clip(at, 0, ids_ref.shape[0] - 1)], -1))

    scaled = dot_nt(xall[:var_count].reshape(var_count * rows, depth), wall[0]).astype(jnp.bfloat16)
    qbuf[...] = scaled * jnp.bfloat16(HD ** (-0.5))
    x_all = xall[...].reshape(count * rows, depth)
    kbuf[...] = dot_nt(x_all, wall[1]).astype(jnp.bfloat16)
    vbuf[...] = dot_nt(x_all, wall[2]).astype(jnp.bfloat16)

    lanes = 128
    lane = lax.broadcasted_iota(jnp.int32, (1, lanes), 1)
    lane_u = lane // heads
    sum_row = lax.broadcasted_iota(jnp.int32, (inner, lanes), 0) // HD
    sum_col = lax.broadcasted_iota(jnp.int32, (inner, lanes), 1)
    spread_row = lax.broadcasted_iota(jnp.int32, (lanes, inner), 0)
    spread_col = lax.broadcasted_iota(jnp.int32, (lanes, inner), 1) // HD
    collect = [(sum_row + u * heads == sum_col).astype(jnp.bfloat16) for u in range(var_count)]
    spread = [(spread_col + u * heads == spread_row).astype(jnp.bfloat16) for u in range(var_count)]
    own_id = jnp.full((1, lanes), -2, jnp.int32)
    for u in range(var_count):
        own_id = jnp.where(lane_u == u, ids[u], own_id)
    reach = [
        [w for w in range(count) if needed(u, w, var_count, far_count)] for u in range(var_count)
    ]
    score = [0.0] * count
    for u in range(var_count):
        query = qbuf[u * rows : (u + 1) * rows, :]
        product = [kbuf[w * rows : (w + 1) * rows, :] * query for w in reach[u]]
        part = jnp.dot(
            jnp.concatenate(product, axis=0), collect[u], preferred_element_type=jnp.float32
        )
        for place, w in enumerate(reach[u]):
            score[w] = score[w] + part[place * rows : (place + 1) * rows]
    scores = [
        jnp.where(own_id == ids[w], score[w], -jnp.inf) for w in range(count)
    ]
    highest = functools.reduce(jnp.maximum, scores)
    highest = jnp.where(lane_u < var_count, highest, 0.0)
    raised = [jnp.exp(one - highest) for one in scores]
    total = functools.reduce(lambda a, b: a + b, raised)
    share = 1.0 / jnp.where(lane_u < var_count, total, 1.0)
    prob = [(one * share).astype(jnp.bfloat16) for one in raised]
    for u in range(var_count):
        shares = jnp.concatenate([prob[w] for w in reach[u]], axis=0)
        each = jnp.dot(shares, spread[u], preferred_element_type=jnp.float32)
        mixed = None
        for place, w in enumerate(reach[u]):
            values = vbuf[w * rows : (w + 1) * rows, :].astype(jnp.float32)
            term = each[place * rows : (place + 1) * rows] * values
            mixed = term if mixed is None else mixed + term
        att[u * rows : (u + 1) * rows, :] = mixed.astype(jnp.bfloat16)
    summed = jnp.dot(att[...], uall[...], preferred_element_type=jnp.float32)
    summed = summed + mid_ref[...].astype(jnp.float32).reshape(summed.shape)
    out_ref[...] = summed.astype(jnp.bfloat16).reshape(out_ref.shape)


def routes(var_size, patch_size):
    def route(even, odd):
        pairs = []
        for v in range(var_size):
            for p in range(patch_size):
                step = odd if v % 2 else even
                pairs.append((v * patch_size + p, v * patch_size + (p ^ step)))
        return pairs
    return route(1, 2), route(2, 1), route(3, 3)


def tied(blocks, after):
    return lax.optimization_barrier((*blocks, after))


def pairs_of(size, partner):
    return [(i, partner(i)) for i in range(size) if 0 <= partner(i) < size]


def on_device(
    tokens, patch_mask, group_ids, time_gain, time_qkv, time_out, space_gain, space_qkv, space_out
):
    var_size, patch_size = lax.axis_size("var"), lax.axis_size("patch")
    var_index, patch_index = lax.axis_index("var"), lax.axis_index("patch")
    core = var_index % 2
    both = ("var", "patch")
    first, second, third = routes(var_size, patch_size)
    swap = pairs_of(var_size, lambda i: i ^ 1)

    def send(block, route):
        return lax.ppermute(block, both, route)

    def partner(block):
        return lax.ppermute(block, "var", swap)

    tok = jnp.transpose(tokens, (1, 0, 2))
    mask = jnp.transpose(patch_mask)
    qkv_t = jnp.transpose(time_qkv, (1, 2, 0))
    qkv_s = jnp.transpose(space_qkv, (1, 2, 0))
    var_count, rows, depth = tok.shape
    kind, width, _ = qkv_t.shape
    half = width // 2

    tok1, tok2 = send(tok, first), send(tok, second)
    mask1, mask2, mask3 = send(mask, first), send(mask, second), send(mask, third)
    tok1f, mask1, mask2, mask3 = lax.optimization_barrier((tok1, mask1, mask2, mask3))
    tok3 = send(tok1f, second)
    weight = qkv_t.reshape(kind * width, depth)
    bf = jnp.bfloat16
    early, marks = pl.pallas_call(
        project_kernel,
        out_shape=[
            jax.ShapeDtypeStruct((3 * var_count * rows, kind * width), bf),
            jax.ShapeDtypeStruct((var_count, patch_size * rows), jnp.int32),
        ],
        in_specs=[VM] * 9,
        out_specs=[VM] * 2,
        compiler_params=params(),
        cost_estimate=cost(1000, 1000),
        name="project",
    )(tok, tok1f, tok2, time_gain, weight, mask, mask1, mask2, mask3)

    far_count = var_count - 1
    level = (var_index // 2) % 2
    place = jnp.stack([core, 1 - level, var_index]).astype(jnp.int32)
    piece = jax.ShapeDtypeStruct((kind + 1, half, depth), bf)
    mine, other = pl.pallas_call(
        split_kernel,
        out_shape=[piece] * 2,
        in_specs=[SM] + [HB] * 2,
        out_specs=[HB] * 2,
        scratch_shapes=[pltpu.SemaphoreType.DMA((4,))],
        compiler_params=params(1),
        cost_estimate=cost(1000, 1000),
        name="split",
    )(place, qkv_s, space_out)
    t_own, mine, other, early = lax.optimization_barrier((time_out[None], mine, other, early))
    t1, c1 = send(t_own, first), send(mine, second)

    near, far_step = jnp.where(core == 0, 1, 2), jnp.where(core == 0, 2, 1)
    bases = jnp.stack(
        [patch_index, patch_index ^ near, patch_index ^ far_step, patch_index ^ 3]
    ).astype(jnp.int32) * rows
    block = jax.ShapeDtypeStruct((var_count, rows, width), bf)
    att = pl.pallas_call(
        time_kernel,
        out_shape=[block, block, jax.ShapeDtypeStruct((2 * var_count, rows, width), bf)],
        in_specs=[SM] + [VM] * 5,
        out_specs=[VM] * 3,
        compiler_params=params(),
        cost_estimate=cost(10_000_000_000, 1000),
        name="time",
    )(bases, early, tok3, marks, time_gain, weight)
    att0, att2, att13 = att
    got = send(att13, first)
    whole = jax.ShapeDtypeStruct((var_count, rows, depth), jnp.bfloat16)
    part = jax.ShapeDtypeStruct((far_count, rows, depth), jnp.bfloat16)
    partial = pl.pallas_call(
        part_kernel,
        out_shape=whole,
        in_specs=[VM] * 4,
        out_specs=VM,
        compiler_params=params(),
        cost_estimate=cost(1000, 1000),
        name="part",
    )(att2, got, time_out, t1)
    partial = send(partial, second)
    mid, x_own = pl.pallas_call(
        mid_kernel,
        out_shape=[whole, whole],
        in_specs=[SM] + [VM] * 7,
        out_specs=[VM] * 2,
        compiler_params=params(),
        cost_estimate=cost(1000, 1000),
        name="mid",
    )(place, att0, got, time_out, t1, partial, tok, space_gain)

    got1 = lax.ppermute(x_own, "var", pairs_of(var_size, lambda i: i ^ 2))
    got2 = lax.ppermute(
        x_own, "var", pairs_of(var_size, lambda i: i + 2 if (i // 2) % 2 else i - 2)
    )
    x_swap = partner(x_own)
    c1f, _ = lax.optimization_barrier((c1, x_own))
    other, _ = lax.optimization_barrier((other, x_own))
    o1 = send(other, second)
    c3 = send(c1f, first)
    swapped1, swapped2 = partner(got1), partner(got2)
    c2 = partner(c1f)
    o1, got1, got2 = lax.optimization_barrier((o1, got1, got2))
    o2 = partner(o1)
    o3 = partner(c3)
    count = 3 * var_count + 2 * far_count
    own_rows = var_count * rows
    inner = 4 * width
    out = pl.pallas_call(
        functools.partial(space_kernel, var_count),
        out_shape=whole,
        in_specs=[SM] * 2 + [VM] * 15,
        out_specs=VM,
        scratch_shapes=[
            pltpu.VMEM((count, rows, depth), bf),
            pltpu.VMEM((kind, inner, depth), bf),
            pltpu.VMEM((inner, depth), bf),
            pltpu.VMEM((own_rows, inner), bf),
            pltpu.VMEM((count * rows, inner), bf),
            pltpu.VMEM((count * rows, inner), bf),
            pltpu.VMEM((own_rows, inner), bf),
        ],
        compiler_params=params(28),
        cost_estimate=cost(1000, 1000),
        name="space",
    )(place, group_ids, x_own, x_swap, got1, got2, swapped1, swapped2, qkv_s, space_out, c1, o1, c2, o2, c3, o3, mid)
    return jnp.transpose(out, (1, 0, 2))


def solution(mesh):
    in_specs = (
        P("patch", ("parts", "var"), None),
        P("patch", ("parts", "var")),
        P("parts"),
        P(),
        P(None, None, "patch"),
        P("patch", None),
        P(),
        P(None, None, "patch"),
        P("patch", None),
    )
    out_specs = P("patch", ("parts", "var"), None)
    return jax.shard_map(
        on_device, mesh=mesh, in_specs=in_specs, out_specs=out_specs, check_vma=False
    )
```
